32 devices in a mesh: groups: 2 (over y), gx: 8 (over z, x), gy: 2 (over core).
Axes of the slice: x: 2, y: 2, z: 4, core: 2. Of those that a mesh axis runs over, the one named last changes fastest.
Arguments:
- tokens: bfloat16 [2, 384, 8192], P(None, ('groups', 'gx'), 'gy'), parts along dimension 1, may hold values from -6 to 6
- gate_up: bfloat16 [2, 8192, 3328], P(None, ('gx', 'gy')), may hold values from -0.0625 to 0.0625
- down_weight: bfloat16 [3328, 8192], P(('gx', 'gy')), may hold values from -0.109375 to 0.109375
Outputs:
- mixed: bfloat16 [2, 384, 8192], P(None, ('groups', 'gx'), 'gy'), parts along dimension 1
The draws below stay inside these ranges and needn't reach their ends.
There are 2 independent parts, one for each index of `groups`. The reference program is written for one: setup_inputs(seed, part) draws one part's arguments, and reference() takes and returns one part's arrays. A program takes and returns all parts, laid end to end along the dimension named above; an argument that names none is the same for every part. Nothing has to cross between parts.
All inputs are finite; a program needn't handle non-finite values.
Results may differ from the reference program's by a relative error of at most 0.005.
Values may be sent and summed in bfloat16 or wider, within the bound.
No kernel may reach another device: no remote copies, remote signals or barrier semaphores. Data moves between devices by JAX's collectives and lax.ppermute only.
A program may use at most 128 MiB of HBM per device.

```python
import jax
import jax.numpy as jnp

D = 8192
ROWS = 192
MB = 2
FF = 3328


def steps_of(rng, shape, cuts, least, high):
    gain, own = 1.0, jax.random.fold_in(rng, 6)
    for dim, shards_of in cuts:
        steps = jnp.exp(jax.random.uniform(jax.random.fold_in(own, dim), (shards_of,), jnp.float32, least / len(cuts), high / len(cuts)))
        gain = gain * jnp.repeat(steps, shape[dim] // shards_of).reshape([-1 if axis == dim else 1 for axis in range(len(shape))])
    return gain


def bell_draw(rng, extent, spread, most, split=(), kind=jnp.bfloat16):
    result = jax.random.normal(rng, extent, jnp.float32) * spread
    if len(split) > 0:
        result = steps_of(rng, extent, split, -0.22, 0.18) * result
    return jnp.clip(result, min=-most, max=most).astype(kind)


def setup_inputs(seed: int = 0, part: int = 0) -> dict:
    splits = jax.random.split(jax.random.key(seed), 4)
    part_keys = jax.random.split(jax.random.fold_in(splits[3], part), 4)
    tokens = bell_draw(part_keys[0], (MB, ROWS, D), 1.0, 6.0, ((1, 8), (2, 2)))
    gate_up = bell_draw(splits[1], (2, D, FF), D ** -0.5, 0.0625, ((1, 16),))
    down_weight = bell_draw(splits[2], (FF, D), FF ** -0.5, 0.109375, ((0, 16),))
    return {"tokens": tokens, "gate_up": gate_up, "down_weight": down_weight}


def reference(tokens, gate_up, down_weight):
    results = []
    for index in range(MB):
        rows_in = tokens[index]
        gate = jnp.dot(rows_in, gate_up[0], preferred_element_type=jnp.float32)
        upper = jnp.dot(rows_in, gate_up[1], preferred_element_type=jnp.float32)
        hidden = (jax.nn.silu(gate) * upper).astype(jnp.bfloat16)
        results.append(jnp.dot(hidden, down_weight, preferred_element_type=jnp.float32).astype(jnp.bfloat16))
    return jnp.stack(results)
```

```python
import functools

import jax
import jax.numpy as jnp
from jax import lax
from jax.experimental import pallas as pl
from jax.experimental.pallas import tpu as pltpu
from jax.sharding import PartitionSpec as P

LANES = 128
QUAD = 4
VMEM = 56 * 1024 * 1024


def wire_type(stage, stages):
    return jnp.bfloat16 if stages - stage <= 3 else jnp.float32


def place(relative, order, send, keep, value):
    first = (relative >> order[0]) & 1
    second = (relative >> order[1]) & 1
    group = 0 if send.shape[0] == 1 else relative >> 2

    @pl.when(first == 1)
    def _():
        send[group, second] = value.astype(send.dtype)

    @pl.when(first == 0)
    def _():
        keep[group, second] = value


def project_kernel(block, chunks, place_ref, tokens, own, other, *refs):
    outs, acc = refs[:-1], refs[-1]
    chip, core = place_ref[0], place_ref[1]
    rows = tokens.shape[1]
    for half in range(2):
        acc[half] = jnp.dot(
            tokens[core], own[half], preferred_element_type=jnp.float32
        ) + jnp.dot(tokens[1 - core], other[half], preferred_element_type=jnp.float32)
    whole_tiles, rest = block // LANES, block % LANES
    fold = LANES // rest
    for q in range(QUAD):
        relative = (q ^ (chip & (QUAD - 1)))
        start = 0
        for index, (count, order) in enumerate(chunks):
            lane = lax.broadcasted_iota(jnp.int32, (count, LANES), 1)
            part = count // fold
            pieces = []
            for half in range(2):
                tile = lambda t, a, n: acc[half, a : a + n, t * LANES : (t + 1) * LANES]
                base = q * block
                shift = base % LANES
                for piece in range(whole_tiles):
                    at = base // LANES + piece
                    value = tile(at, start, count)
                    if shift:
                        value = jnp.where(lane < shift, tile(at + 1, start, count), value)
                        value = pltpu.roll(value, LANES - shift, 1)
                    pieces.append(value)
                last = base + whole_tiles * LANES
                packed = None
                for k in range(fold):
                    value = tile(last // LANES, start + k * part, part)
                    turn = (k * rest - last % LANES) % LANES
                    if turn:
                        value = pltpu.roll(value, turn, 1)
                    packed = value if k == 0 else jnp.where(lane[:part] < k * rest, packed, value)
                pieces.append(packed)
            place(relative, order, outs[2 * index], outs[2 * index + 1], jnp.concatenate(pieces, axis=0))
            start += count


def project(spot, tokens, own, other, count_x, chunks, stages):
    block = own.shape[2] // count_x
    rows, depth = tokens.shape[1], tokens.shape[2]
    wide = QUAD * block
    groups = count_x // QUAD
    shapes, specs = [], []
    for count, _ in chunks:
        lines = 2 * count * block // LANES
        for kind in (wire_type(0, stages), jnp.float32):
            shapes.append(jax.ShapeDtypeStruct((groups, 2, lines, LANES), kind))
            specs.append(pl.BlockSpec((1, 2, lines, LANES), lambda g, s: (g ^ (s[0] >> 2), 0, 0, 0)))
    weights = pl.BlockSpec((2, depth, wide), lambda g, s: (0, 0, g))
    return pl.pallas_call(
        functools.partial(project_kernel, block, chunks),
        out_shape=shapes,
        grid_spec=pltpu.PrefetchScalarGridSpec(
            num_scalar_prefetch=1,
            grid=(groups,),
            in_specs=[pl.BlockSpec((2, rows, depth), lambda g, s: (0, 0, 0)), weights, weights],
            out_specs=specs,
            scratch_shapes=[pltpu.VMEM((2, rows, wide), jnp.float32)],
        ),
        compiler_params=pltpu.CompilerParams(vmem_limit_bytes=VMEM),
        cost_estimate=pl.CostEstimate(
            flops=8 * rows * depth * own.shape[2], bytes_accessed=4 * own.size, transcendentals=0
        ),
    )(spot, tokens, own, other)


def down_kernel(block, count, order, place_ref, keep_in, recv_in, down, send, keep, hidden):
    chip = place_ref[0]
    whole_tiles, rest = block // LANES, block % LANES
    fold = LANES // rest

    @pl.when(pl.program_id(0) == 0)
    def _():
        sums = keep_in[...] + recv_in[...].astype(jnp.float32)
        lines = sums.shape[0] // 2
        gate, upper = sums[:lines], sums[lines:]
        value = gate / (1.0 + jnp.exp(-gate)) * upper
        for piece in range(whole_tiles):
            hidden[:, piece * LANES : (piece + 1) * LANES] = value[
                piece * count : (piece + 1) * count
            ].astype(jnp.bfloat16)
        packed = value[whole_tiles * count :]
        part = count // fold
        for k in range(fold):
            turned = pltpu.roll(packed, (LANES - k * rest) % LANES, 1) if k else packed
            hidden[k * part : (k + 1) * part, whole_tiles * LANES :] = turned[:, :rest].astype(jnp.bfloat16)

    product = jnp.dot(hidden[...], down[...], preferred_element_type=jnp.float32)
    chips = 4 * send.shape[0]
    each = count // chips
    for owner in range(chips):
        place(owner ^ chip, order, send, keep, product[owner * each : (owner + 1) * each])


def down_project(spot, keep, recv, down, count, order, count_x, stages, wide=2048):
    block, features = down.shape
    groups = count_x // QUAD
    each = count // count_x
    lines = keep.shape[0]
    whole = pl.BlockSpec((lines, LANES), lambda c, s: (0, 0))
    out = pl.BlockSpec((groups, 2, each, wide), lambda c, s: (0, 0, 0, c))
    return pl.pallas_call(
        functools.partial(down_kernel, block, count, order),
        out_shape=[
            jax.ShapeDtypeStruct((groups, 2, each, features), kind)
            for kind in (wire_type(0, stages), jnp.float32)
        ],
        grid_spec=pltpu.PrefetchScalarGridSpec(
            num_scalar_prefetch=1,
            grid=(features // wide,),
            in_specs=[whole, whole, pl.BlockSpec((block, wide), lambda c, s: (0, c))],
            out_specs=[out, out],
            scratch_shapes=[pltpu.VMEM((count, block), jnp.bfloat16)],
        ),
        compiler_params=pltpu.CompilerParams(vmem_limit_bytes=VMEM),
        cost_estimate=pl.CostEstimate(
            flops=2 * count * block * features, bytes_accessed=2 * down.size, transcendentals=0
        ),
    )(spot, keep, recv, down)


def reduce_stages(send, keep, order, count_x, stages):
    swap = lambda value, bit: lax.ppermute(value, "gx", [(i, i ^ (1 << bit)) for i in range(count_x)])
    recv = swap(send, order[0])
    acc = keep + recv.astype(jnp.float32)
    send, keep = acc[:, 1].astype(wire_type(1, stages)), acc[:, 0]
    recv = swap(send, order[1])
    for stage in range(2, stages):
        acc = keep + recv.astype(jnp.float32)
        half = acc.shape[0] // 2
        send, keep = acc[half:].astype(wire_type(stage, stages)), acc[:half]
        recv = swap(send, 2 + half.bit_length() - 1)
    return keep[0], recv[0]


def swap_cores(value):
    return lax.ppermute(value, "gy", [(0, 1), (1, 0)])


def local(tokens, gate_up, down_weight):
    count_x = lax.axis_size("gx")
    stages = count_x.bit_length() - 1
    chip, core = lax.axis_index("gx"), lax.axis_index("gy")
    spot = jnp.stack([chip, core]).astype(jnp.int32)
    each, features = tokens.shape[1], tokens.shape[2]
    depth = gate_up.shape[1]

    mine = lax.dynamic_index_in_dim(tokens, core, 0, False)
    theirs = swap_cores(lax.dynamic_index_in_dim(tokens, 1 - core, 0, False))
    rows = jnp.where(core == 0, jnp.stack([mine, theirs]), jnp.stack([theirs, mine]))
    rows = rows.reshape(2, each, count_x // 2, 2 * depth).transpose(0, 2, 1, 3)
    rows = rows.reshape(count_x, each, 2 * depth)
    other = swap_cores(gate_up)
    down_other = swap_cores(down_weight)
    rows = lax.all_to_all(rows, "gx", 0, 0)

    cuts = [(0, 16, (0, 1)), (16, 24, (1, 0))] if each % 8 == 0 and each > 16 else [(0, each, (0, 1))]
    chunks = tuple((count_x * (b - a), order) for a, b, order in cuts)
    rows = jnp.concatenate([rows[:, a:b].reshape(count_x * (b - a), 2 * depth) for a, b, _ in cuts])
    rows = rows.reshape(-1, 2, depth).transpose(1, 0, 2)
    down = jnp.where(
        core == 0,
        jnp.concatenate([down_weight, down_other]),
        jnp.concatenate([down_other, down_weight]),
    )
    parts = project(spot, rows, gate_up, other, count_x, chunks, stages)
    results = []
    for index, (count, order) in enumerate(chunks):
        keep, recv = reduce_stages(parts[2 * index], parts[2 * index + 1], order, count_x, stages)
        send, keep = down_project(spot, keep, recv, down, count, order, count_x, stages)
        keep, recv = reduce_stages(send, keep, order, count_x, stages)
        mixed = (keep + recv.astype(jnp.float32)).astype(jnp.bfloat16)
        halves = mixed.reshape(mixed.shape[0], 2, features)
        mine = lax.dynamic_index_in_dim(halves, core, 1, False)
        theirs = swap_cores(lax.dynamic_index_in_dim(halves, 1 - core, 1, False))
        results.append(jnp.where(core == 0, jnp.stack([mine, theirs]), jnp.stack([theirs, mine])))
    return jnp.concatenate(results, axis=1)


def solution(mesh):
    return jax.shard_map(
        local,
        mesh=mesh,
        in_specs=(
            P(None, ("groups", "gx"), "gy"),
            P(None, ("gx", "gy"), None),
            P(("gx", "gy"), None),
        ),
        out_specs=P(None, ("groups", "gx"), "gy"),
        check_vma=False,
    )
```

```python
import functools

import jax
import jax.numpy as jnp
from jax import lax
from jax.experimental import pallas as pl
from jax.experimental.pallas import tpu as pltpu
from jax.sharding import PartitionSpec as P

LANES = 128
QUAD = 4
VMEM = 56 * 1024 * 1024


def wire_type(stage, stages):
    return jnp.bfloat16 if stages - stage <= 3 else jnp.float32


def place(relative, order, send, keep, value):
    first = (relative >> order[0]) & 1
    second = (relative >> order[1]) & 1
    group = 0 if send.shape[0] == 1 else relative >> 2

    @pl.when(first == 1)
    def _():
        send[group, second] = value.astype(send.dtype)

    @pl.when(first == 0)
    def _():
        keep[group, second] = value


def project_kernel(block, cuts, place_ref, tokens, own, other, *refs):
    outs, acc = refs[:-1], refs[-1]
    chip, core = place_ref[0], place_ref[1]
    chips, each = tokens.shape[0] // cuts[-1][1], cuts[-1][1]
    depth = own.shape[1]
    low, high = tokens[:, :depth], tokens[:, depth:]
    acc[...] = jnp.dot(
        jnp.where(core == 0, low, high), own[0], preferred_element_type=jnp.float32
    ) + jnp.dot(jnp.where(core == 0, high, low), other[0], preferred_element_type=jnp.float32)
    whole_tiles, rest = block // LANES, block % LANES
    fold = LANES // rest
    for index, (first, last, order) in enumerate(cuts):
        count = chips * (last - first)
        part = count // fold
        lane = lax.broadcasted_iota(jnp.int32, (count, LANES), 1)

        def tile(at):
            lanes = slice(at * LANES, (at + 1) * LANES)
            if count == tokens.shape[0]:
                return acc[:, lanes]
            return jnp.concatenate(
                [acc[chip * each + first : chip * each + last, lanes] for chip in range(chips)]
            )

        for q in range(QUAD):
            base = q * block
            shift = base % LANES
            pieces = []
            for piece in range(whole_tiles):
                at = base // LANES + piece
                value = tile(at)
                if shift:
                    value = jnp.where(lane < shift, tile(at + 1), value)
                    value = pltpu.roll(value, LANES - shift, 1)
                pieces.append(value)
            tail = base + whole_tiles * LANES
            rests = tile(tail // LANES)
            packed = None
            for k in range(fold):
                value = rests[k * part : (k + 1) * part]
                turn = (k * rest - tail % LANES) % LANES
                if turn:
                    value = pltpu.roll(value, turn, 1)
                packed = value if k == 0 else jnp.where(lane[:part] < k * rest, packed, value)
            pieces.append(packed)
            place(
                q ^ (chip & (QUAD - 1)),
                order,
                outs[2 * index],
                outs[2 * index + 1],
                jnp.concatenate(pieces),
            )


def project(spot, tokens, own, other, count_x, cuts, stages):
    block = own.shape[2] // count_x
    rows, depth = tokens.shape[0], own.shape[1]
    wide = QUAD * block
    groups = count_x // QUAD
    shapes, specs = [], []
    for first, last, _ in cuts:
        lines = count_x * (last - first) * block // LANES
        for kind in (wire_type(0, stages), jnp.float32):
            shapes.append(jax.ShapeDtypeStruct((groups, 2, 2, lines, LANES), kind))
            specs.append(
                pl.BlockSpec((1, 2, None, lines, LANES), lambda g, h, s: (g ^ (s[0] >> 2), 0, h, 0, 0))
            )
    weights = pl.BlockSpec((1, depth, wide), lambda g, h, s: (h, 0, g))
    return pl.pallas_call(
        functools.partial(project_kernel, block, cuts),
        out_shape=shapes,
        grid_spec=pltpu.PrefetchScalarGridSpec(
            num_scalar_prefetch=1,
            grid=(groups, 2),
            in_specs=[pl.BlockSpec(tokens.shape, lambda g, h, s: (0, 0)), weights, weights],
            out_specs=specs,
            scratch_shapes=[pltpu.VMEM((rows, wide), jnp.float32)],
        ),
        compiler_params=pltpu.CompilerParams(vmem_limit_bytes=VMEM),
        cost_estimate=pl.CostEstimate(
            flops=8 * rows * depth * own.shape[2], bytes_accessed=4 * own.size, transcendentals=0
        ),
    )(spot, tokens, own, other)


def down_kernel(block, count, order, place_ref, keep_in, recv_in, down, send, keep, hidden):
    chip = place_ref[0]
    whole_tiles, rest = block // LANES, block % LANES
    fold = LANES // rest

    @pl.when(pl.program_id(0) == 0)
    def _():
        gate = keep_in[0] + recv_in[0].astype(jnp.float32)
        upper = keep_in[1] + recv_in[1].astype(jnp.float32)
        value = gate / (1.0 + jnp.exp(-gate)) * upper
        for piece in range(whole_tiles):
            hidden[:, piece * LANES : (piece + 1) * LANES] = value[
                piece * count : (piece + 1) * count
            ].astype(jnp.bfloat16)
        packed = value[whole_tiles * count :]
        part = count // fold
        for k in range(fold):
            turned = pltpu.roll(packed, (LANES - k * rest) % LANES, 1) if k else packed
            hidden[k * part : (k + 1) * part, whole_tiles * LANES :] = turned[:, :rest].astype(jnp.bfloat16)

    product = jnp.dot(hidden[...], down[...], preferred_element_type=jnp.float32)
    chips = 4 * send.shape[0]
    each = count // chips
    for owner in range(chips):
        place(owner ^ chip, order, send, keep, product[owner * each : (owner + 1) * each])


def down_project(spot, keep, recv, down, count, order, count_x, stages, span=(0, 1), wide=2048):
    block, features = down.shape
    part, parts = span
    features = features // parts
    wide = min(wide, features)
    groups = count_x // QUAD
    each = count // count_x
    whole = pl.BlockSpec(keep.shape, lambda c, s: (0, 0, 0))
    out = pl.BlockSpec((groups, 2, each, wide), lambda c, s: (0, 0, 0, c))
    return pl.pallas_call(
        functools.partial(down_kernel, block, count, order),
        out_shape=[
            jax.ShapeDtypeStruct((groups, 2, each, features), kind)
            for kind in (wire_type(0, stages), jnp.float32)
        ],
        grid_spec=pltpu.PrefetchScalarGridSpec(
            num_scalar_prefetch=1,
            grid=(features // wide,),
            in_specs=[
                whole,
                whole,
                pl.BlockSpec((block, wide), lambda c, s: (0, part * (features // wide) + c)),
            ],
            out_specs=[out, out],
            scratch_shapes=[pltpu.VMEM((count, block), jnp.bfloat16)],
        ),
        compiler_params=pltpu.CompilerParams(vmem_limit_bytes=VMEM),
        cost_estimate=pl.CostEstimate(
            flops=2 * count * block * features, bytes_accessed=2 * block * features, transcendentals=0
        ),
    )(spot, keep, recv, down)


def swap(value, bit):
    count = lax.axis_size("gx")
    return lax.ppermute(value, "gx", [(i, i ^ (1 << bit)) for i in range(count)])


def swap_cores(value):
    return lax.ppermute(value, "gy", [(0, 1), (1, 0)])


def after(value, done):
    return value if done is None else lax.optimization_barrier((value, done))[0]


def halving(send, keep, order, stages, done, narrow_last=True):
    recv = swap(send, order[0])
    done = yield send
    for stage in range(1, stages):
        acc = keep + after(recv, done).astype(jnp.float32)
        kind = wire_type(stage, stages)
        if stage == stages - 1 and not narrow_last:
            kind = jnp.float32
        if stage == 1:
            send, keep, bit = acc[:, 1].astype(kind), acc[:, 0], order[1]
        else:
            half = acc.shape[0] // 2
            send, keep, bit = acc[half:].astype(kind), acc[:half], 1 + half.bit_length()
        recv = swap(send, bit)
        done = yield send
    return keep[0], after(recv, done)[0]


def chunk_steps(spot, parts, down, cut, count_x, stages, narrow_last):
    first, last, order = cut
    core = spot[1]
    keep, recv = yield from halving(parts[0], parts[1], order, stages, None, narrow_last)
    count = count_x * (last - first)
    send, keep = down_project(spot, keep, recv, down, count, order, count_x, stages)
    keep, recv = yield from halving(send, keep, order, stages, None)
    mixed = (keep + recv.astype(jnp.float32)).astype(jnp.bfloat16)
    halves = mixed.reshape(mixed.shape[0], 2, -1)
    mine = lax.dynamic_index_in_dim(halves, core, 1, False)
    send = lax.dynamic_index_in_dim(halves, 1 - core, 1, False)
    theirs = swap_cores(send)
    yield send
    return jnp.where(core == 0, jnp.stack([mine, theirs]), jnp.stack([theirs, mine]))


def local(tokens, gate_up, down_weight):
    count_x = lax.axis_size("gx")
    stages = count_x.bit_length() - 1
    chip, core = lax.axis_index("gx"), lax.axis_index("gy")
    spot = jnp.stack([chip, core]).astype(jnp.int32)
    each = tokens.shape[1]
    depth = gate_up.shape[1]

    mine = lax.dynamic_index_in_dim(tokens, core, 0, False)
    theirs = swap_cores(lax.dynamic_index_in_dim(tokens, 1 - core, 0, False))
    other = swap_cores(after(gate_up, theirs))
    down_other = swap_cores(after(down_weight, theirs))
    rows = jnp.where(core == 0, jnp.stack([mine, theirs]), jnp.stack([theirs, mine]))
    rows = rows.reshape(2, each, count_x // 2, 2 * depth).transpose(0, 2, 1, 3)
    rows = rows.reshape(count_x, each, 2 * depth)
    rows = lax.all_to_all(rows, "gx", 0, 0).reshape(count_x * each, 2 * depth)

    step = 8 if each % 8 == 0 else each
    cuts = tuple((a, a + step, (0, 1)) for a in range(0, each, step))
    down = jnp.where(
        core == 0,
        jnp.concatenate([down_weight, down_other]),
        jnp.concatenate([down_other, down_weight]),
    )
    parts = project(spot, rows, gate_up, other, count_x, cuts, stages)
    chunks = [
        chunk_steps(spot, parts[2 * i : 2 * i + 2], down, cut, count_x, stages, i == 0)
        for i, cut in enumerate(cuts)
    ]
    turns = sorted((turn + 1.6 * i, i) for i in range(len(cuts)) for turn in range(2 * stages + 2))
    done, results = None, {}
    for _, i in turns:
        try:
            done = chunks[i].send(done if i in results else None)
            results[i] = None
        except StopIteration as end:
            results[i] = end.value
    return jnp.concatenate([results[i] for i in range(len(cuts))], axis=1)


def solution(mesh):
    return jax.shard_map(
        local,
        mesh=mesh,
        in_specs=(
            P(None, ("groups", "gx"), "gy"),
            P(None, ("gx", "gy"), None),
            P(("gx", "gy"), None),
        ),
        out_specs=P(None, ("groups", "gx"), "gy"),
        check_vma=False,
    )
```

```python
import functools

import jax
import jax.numpy as jnp
from jax import lax
from jax.experimental import pallas as pl
from jax.experimental.pallas import tpu as pltpu
from jax.sharding import PartitionSpec as P

LANES = 128
QUAD = 4
VMEM = 20 * 1024 * 1024


ORDERS = [((0, 1), (0, 1)), ((1, 0), (1, 0)), ((0, 1), (1, 0))]
TURNS = [0, 1, 0, 1, 2, 0, 1, 0, 2, 1, 2, 0, 2, 1, 0, 1, 0, 2, 1, 0, 2, 1, 2, 2]


def wire_type(stage, stages):
    return jnp.bfloat16 if stages - stage <= 3 else jnp.float32


def place(relative, order, send, keep, value):
    first = (relative >> order[0]) & 1
    second = (relative >> order[1]) & 1
    group = 0 if send.shape[0] == 1 else relative >> 2

    @pl.when(first == 1)
    def _():
        send[group, second] = value.astype(send.dtype)

    @pl.when(first == 0)
    def _():
        keep[group, second] = value


def project_kernel(block, cuts, place_ref, tokens, own_in, other_in, *refs):
    outs, (own, other, accs, sems) = refs[:-4], refs[-4:]
    chip, core = place_ref[0], place_ref[1]
    chips, each = tokens.shape[0] // cuts[-1][1], cuts[-1][1]
    halves, depth, wide = own.shape[0], own.shape[1], QUAD * block
    groups = own.shape[2] // wide
    span = wide if groups <= 2 else own.shape[2]
    loads = {}
    for half in range(halves):
        for group in range(own.shape[2] // span):
            lanes = slice(group * span, (group + 1) * span)
            loads[half, group] = [
                pltpu.make_async_copy(source.at[half, :, lanes], target.at[half, :, lanes], sems.at[i, half, group])
                for i, (source, target) in enumerate(((own_in, own), (other_in, other)))
            ]
            for load in loads[half, group]:
                load.start()
    low, high = tokens[:, :depth], tokens[:, depth:]
    first_rows = jnp.where(core == 0, low, high)
    second_rows = jnp.where(core == 0, high, low)
    whole_tiles, rest = block // LANES, block % LANES
    fold = LANES // rest

    def step(half, group, acc):
        at = group * wide
        span = pl.ds(at if isinstance(at, int) else pl.multiple_of(at, LANES), wide)
        acc[...] = jnp.dot(first_rows, own[half, :, span], preferred_element_type=jnp.float32) + jnp.dot(
            second_rows, other[half, :, span], preferred_element_type=jnp.float32
        )
        for index, (first, last, order) in enumerate(cuts):
            count = chips * (last - first)
            part = count // fold
            lane = lax.broadcasted_iota(jnp.int32, (count, LANES), 1)

            def tile(at):
                lanes = slice(at * LANES, (at + 1) * LANES)
                if count == tokens.shape[0]:
                    return acc[:, lanes]
                return jnp.concatenate([acc[c * each + first : c * each + last, lanes] for c in range(chips)])

            for q in range(QUAD):
                base, shift = q * block // LANES, q * block % LANES
                tail = tile(base + whole_tiles)
                head = tile(base)
                pieces = [jnp.where(lane < shift, tail, head) if shift else head]
                pieces += [tile(base + t) for t in range(1, whole_tiles)]
                packed = None
                for k in range(fold):
                    value = tail[k * part : (k + 1) * part]
                    turn = (k * rest - shift) % LANES
                    if turn:
                        value = pltpu.roll(value, turn, 1)
                    packed = value if k == 0 else jnp.where(lane[:part] < k * rest, packed, value)
                pieces.append(packed)
                value = jnp.concatenate(pieces)
                relative = (QUAD * group + q) ^ chip
                outer, a, b = relative >> 2, (relative >> order[0]) & 1, (relative >> order[1]) & 1
                send, keep = outs[2 * index], outs[2 * index + 1]

                @pl.when(a == 1)
                def _():
                    send[outer, b, half] = value.astype(send.dtype)

                @pl.when(a == 0)
                def _():
                    keep[outer, b, half] = value

    for half in range(halves):
        for group in range(own.shape[2] // span):
            for load in loads[half, group]:
                load.wait()
            if groups <= 2:
                step(half, group, accs.at[group % 2])
            else:
                lax.fori_loop(0, groups, lambda g, c: step(half, g, accs.at[0]), None)


def project(spot, tokens, own, other, count_x, cuts, stages):
    block = own.shape[2] // count_x
    rows, depth = tokens.shape[0], own.shape[1]
    groups = count_x // QUAD
    if groups > 2 and own.shape[0] > 1:
        two = [project(spot, tokens, own[h : h + 1], other[h : h + 1], count_x, cuts, stages) for h in range(2)]
        return [jnp.concatenate(pair, axis=2) for pair in zip(*two)]
    shapes = []
    for first, last, _ in cuts:
        lines = count_x * (last - first) * block // LANES
        for kind in (wire_type(0, stages), jnp.float32):
            shapes.append(jax.ShapeDtypeStruct((groups, 2, own.shape[0], lines, LANES), kind))
    inside = pl.BlockSpec(memory_space=pltpu.VMEM)
    scratch = jax.ShapeDtypeStruct((2, rows, QUAD * block), jnp.float32)
    held = sum(t.size * t.dtype.itemsize for t in [tokens, own, other, scratch, *shapes])
    return pl.pallas_call(
        functools.partial(project_kernel, block, cuts),
        out_shape=shapes,
        in_specs=[pl.BlockSpec(memory_space=pltpu.SMEM), inside] + [pl.BlockSpec(memory_space=pltpu.HBM)] * 2,
        out_specs=[inside] * len(shapes),
        scratch_shapes=[
            pltpu.VMEM(own.shape, own.dtype),
            pltpu.VMEM(own.shape, own.dtype),
            pltpu.VMEM(scratch.shape, scratch.dtype),
            pltpu.SemaphoreType.DMA((2, own.shape[0], 2)),
        ],
        compiler_params=pltpu.CompilerParams(vmem_limit_bytes=held + 4 * 1024 * 1024),
        cost_estimate=pl.CostEstimate(
            flops=4 * rows * depth * own.shape[2], bytes_accessed=2 * own.size, transcendentals=0
        ),
    )(spot, tokens, own, other)


def down_kernel(block, count, order, place_ref, keep_in, recv_in, own, other, send, keep, hidden):
    chip, core = place_ref[0], place_ref[1]
    whole_tiles, rest = block // LANES, block % LANES
    fold = LANES // rest

    @pl.when(pl.program_id(0) == 0)
    def _():
        gate = keep_in[0] + recv_in[0].astype(jnp.float32)
        upper = keep_in[1] + recv_in[1].astype(jnp.float32)
        value = gate / (1.0 + jnp.exp(-gate)) * upper
        tiles = jnp.concatenate(
            [value[piece * count : (piece + 1) * count] for piece in range(whole_tiles)], axis=1
        )
        shift = (chip & (QUAD - 1)) * rest
        turned = pltpu.roll(tiles, lax.rem(whole_tiles * LANES - shift, whole_tiles * LANES), 1)
        high = turned.astype(jnp.bfloat16)
        hidden[:count, : whole_tiles * LANES] = high
        hidden[count:, : whole_tiles * LANES] = (turned - high.astype(jnp.float32)).astype(jnp.bfloat16)
        packed = value[whole_tiles * count :]
        part = count // fold
        for k in range(fold):
            turned = pltpu.roll(packed, (LANES - k * rest) % LANES, 1) if k else packed
            turned = turned[:, :rest]
            high = turned.astype(jnp.bfloat16)
            hidden[k * part : (k + 1) * part, whole_tiles * LANES :] = high
            hidden[count + k * part : count + (k + 1) * part, whole_tiles * LANES :] = (
                turned - high.astype(jnp.float32)
            ).astype(jnp.bfloat16)

    low, high = hidden[:, : block // 2], hidden[:, block // 2 :]
    product = jnp.dot(
        jnp.where(core == 0, low, high), own[...], preferred_element_type=jnp.float32
    ) + jnp.dot(jnp.where(core == 0, high, low), other[...], preferred_element_type=jnp.float32)
    product = product[:count] + product[count:]
    chips = 4 * send.shape[0]
    each = count // chips
    for owner in range(chips):
        place(owner ^ chip, order, send, keep, product[owner * each : (owner + 1) * each])


def down_project(spot, keep, recv, own, other, count, order, count_x, stages, span=(0, 1), wide=4096):
    block, features = 2 * own.shape[0], own.shape[1]
    part, parts = span
    features = features // parts
    wide = min(wide, features)
    groups = count_x // QUAD
    each = count // count_x
    whole = pl.BlockSpec(keep.shape, lambda c, s: (0, 0, 0))
    out = pl.BlockSpec((groups, 2, each, wide), lambda c, s: (0, 0, 0, c))
    weights = pl.BlockSpec((block // 2, wide), lambda c, s: (0, part * (features // wide) + c))
    return pl.pallas_call(
        functools.partial(down_kernel, block, count, order),
        out_shape=[
            jax.ShapeDtypeStruct((groups, 2, each, features), kind)
            for kind in (wire_type(0, stages), jnp.float32)
        ],
        grid_spec=pltpu.PrefetchScalarGridSpec(
            num_scalar_prefetch=1,
            grid=(features // wide,),
            in_specs=[
                whole,
                whole,
                weights,
                weights,
            ],
            out_specs=[out, out],
            scratch_shapes=[pltpu.VMEM((2 * count, block), jnp.bfloat16)],
        ),
        compiler_params=pltpu.CompilerParams(vmem_limit_bytes=VMEM),
        cost_estimate=pl.CostEstimate(
            flops=2 * count * block * features, bytes_accessed=2 * block * features, transcendentals=0
        ),
    )(spot, keep, recv, own, other)


def swap(value, bit):
    count = lax.axis_size("gx")
    return lax.ppermute(value, "gx", [(i, i ^ (1 << bit)) for i in range(count)])


def swap_cores(value):
    return lax.ppermute(value, "gy", [(0, 1), (1, 0)])


def after(value, done):
    return value if done is None else lax.optimization_barrier((value, done))[0]


def halving(send, keep, order, stages, done):
    recv = swap(after(send, done), order[0])
    done = yield send
    for stage in range(1, stages):
        acc = keep + after(recv, done).astype(jnp.float32)
        kind = wire_type(stage, stages)
        if stage == 1:
            send, keep, bit = acc[:, 1].astype(kind), acc[:, 0], order[1]
        else:
            half = acc.shape[0] // 2
            send, keep, bit = acc[half:].astype(kind), acc[:half], 1 + half.bit_length()
        recv = swap(send, bit)
        done = yield send
    return keep[0], after(recv, done)[0]


def chunk_steps(spot, parts, downs, count, orders, count_x, stages):
    core = spot[1]
    done = yield
    keep, recv = yield from halving(parts[0], parts[1], orders[0], stages, done)
    send, keep = down_project(spot, keep, recv, *downs, count, orders[1], count_x, stages)
    keep, recv = yield from halving(send, keep, orders[1], stages, None)
    mixed = (keep + recv.astype(jnp.float32)).astype(jnp.bfloat16)
    halves = mixed.reshape(mixed.shape[0], 2, -1)
    mine = lax.dynamic_index_in_dim(halves, core, 1, False)
    send = lax.dynamic_index_in_dim(halves, 1 - core, 1, False)
    theirs = swap_cores(send)
    done = yield send
    theirs = after(theirs, done)
    return jnp.where(core == 0, jnp.stack([mine, theirs]), jnp.stack([theirs, mine]))


def local(tokens, gate_up, down_weight):
    count_x = lax.axis_size("gx")
    stages = count_x.bit_length() - 1
    chip, core = lax.axis_index("gx"), lax.axis_index("gy")
    spot = jnp.stack([chip, core]).astype(jnp.int32)
    each = tokens.shape[1]
    depth = gate_up.shape[1]

    mine = lax.dynamic_index_in_dim(tokens, core, 0, False)
    theirs = swap_cores(lax.dynamic_index_in_dim(tokens, 1 - core, 0, False))
    other = swap_cores(after(gate_up, theirs))
    down_other = swap_cores(after(down_weight, theirs))
    rows = jnp.where(core == 0, jnp.stack([mine, theirs]), jnp.stack([theirs, mine]))
    rows = rows.reshape(2, each, count_x // 2, 2 * depth).transpose(0, 2, 1, 3)
    rows = rows.reshape(count_x, each, 2 * depth)
    rows = lax.all_to_all(rows, "gx", 0, 0).reshape(count_x * each, 2 * depth)

    if stages == 3 and each == 24:
        step, orders, turns = 8, ORDERS, TURNS
    else:
        step, orders = each, [((0, 1), (0, 1))]
        turns = [0] * (2 * stages + 2)
    cuts = tuple((i * step, (i + 1) * step, order[0]) for i, order in enumerate(orders))
    parts = project(spot, rows, gate_up, other, count_x, cuts, stages)
    chunks = [
        chunk_steps(
            spot, parts[2 * i : 2 * i + 2], (down_weight, down_other), count_x * step, order, count_x, stages
        )
        for i, order in enumerate(orders)
    ]
    for chunk in chunks:
        next(chunk)
    done, results = None, {}
    for i in turns:
        try:
            done = chunks[i].send(done)
        except StopIteration as end:
            results[i] = end.value
    return jnp.concatenate([results[i] for i in range(len(cuts))], axis=1)


def solution(mesh):
    return jax.shard_map(
        local,
        mesh=mesh,
        in_specs=(
            P(None, ("groups", "gx"), "gy"),
            P(None, ("gx", "gy"), None),
            P(("gx", "gy"), None),
        ),
        out_specs=P(None, ("groups", "gx"), "gy"),
        check_vma=False,
    )
```

```python
import functools

import jax
import jax.numpy as jnp
from jax import lax
from jax.experimental import pallas as pl
from jax.experimental.pallas import tpu as pltpu
from jax.sharding import PartitionSpec as P

LANES = 128
QUAD = 4


ORDERS = [((0, 1), (0, 1)), ((1, 0), (1, 0)), ((0, 1), (1, 0))]
TURNS = [0, 1, 0, 1, 2, 0, 1, 0, 2, 1, 2, 0, 2, 1, 0, 1, 0, 2, 1, 0, 2, 1, 2, 2]


def wire_type(stage, stages):
    return jnp.bfloat16 if stages - stage <= 3 else jnp.float32


def place(relative, order, send, keep, value):
    first = (relative >> order[0]) & 1
    second = (relative >> order[1]) & 1
    group = 0 if send.shape[1] == 1 else relative >> 2

    @pl.when(first == 1)
    def _():
        send[second, group] = value.astype(send.dtype)

    @pl.when(first == 0)
    def _():
        keep[second, group] = value


def deal_kernel(place_ref, tokens, *messages):
    count, wide = len(messages), messages[0].shape[1]
    for turn, message in enumerate(messages):
        target = lax.rem(place_ref[0] + turn, count)
        message[...] = tokens[:, pl.ds(pl.multiple_of(target * wide, LANES), wide)]


def deal(spot, tokens, count):
    rows, features = tokens.shape
    inside = pl.BlockSpec(memory_space=pltpu.VMEM)
    return pl.pallas_call(
        deal_kernel,
        out_shape=[jax.ShapeDtypeStruct((rows, features // count), tokens.dtype)] * count,
        in_specs=[pl.BlockSpec(memory_space=pltpu.SMEM), inside],
        out_specs=[inside] * count,
        compiler_params=pltpu.CompilerParams(vmem_limit_bytes=8 * 1024 * 1024),
    )(spot, tokens)


def project_kernel(block, cuts, messages, place_ref, *refs):
    arrived, own_in, other_in = refs[:messages], refs[messages], refs[messages + 1]
    outs, (tokens, own, other, accs, sems) = refs[messages + 2 : -5], refs[-5:]
    chip, core = place_ref[0], place_ref[1]
    chips, each = tokens.shape[0] // cuts[-1][1], cuts[-1][1]
    halves, depth, wide = own.shape[0], own.shape[1], QUAD * block
    groups = own.shape[2] // wide
    span = wide if groups <= 2 else own.shape[2]
    loads = {}
    for half in range(halves):
        for group in range(own.shape[2] // span):
            lanes = slice(group * span, (group + 1) * span)
            loads[half, group] = [
                pltpu.make_async_copy(source.at[half, :, lanes], target.at[half, :, lanes], sems.at[i, half, group])
                for i, (source, target) in enumerate(((own_in, own), (other_in, other)))
            ]
            for load in loads[half, group]:
                load.start()
    size = arrived[0].shape[0]
    for turn, message in enumerate(arrived):
        source = lax.rem(chip + messages - turn, messages) if messages > 1 else 0
        tokens[pl.ds(pl.multiple_of(source * size, size), size), :] = message[...]
    low, high = tokens[:, :depth], tokens[:, depth:]
    first_rows = jnp.where(core == 0, low, high)
    second_rows = jnp.where(core == 0, high, low)
    whole_tiles, rest = block // LANES, block % LANES
    fold = LANES // rest

    def step(half, group, acc):
        at = group * wide
        span = pl.ds(at if isinstance(at, int) else pl.multiple_of(at, LANES), wide)
        acc[...] = jnp.dot(first_rows, own[half, :, span], preferred_element_type=jnp.float32) + jnp.dot(
            second_rows, other[half, :, span], preferred_element_type=jnp.float32
        )
        for index, (first, last, order) in enumerate(cuts):
            count = chips * (last - first)
            part = count // fold
            lane = lax.broadcasted_iota(jnp.int32, (count, LANES), 1)

            def tile(at):
                lanes = slice(at * LANES, (at + 1) * LANES)
                if count == tokens.shape[0]:
                    return acc[:, lanes]
                return jnp.concatenate([acc[c * each + first : c * each + last, lanes] for c in range(chips)])

            for q in range(QUAD):
                base, shift = q * block // LANES, q * block % LANES
                tail = tile(base + whole_tiles)
                head = tile(base)
                pieces = [jnp.where(lane < shift, tail, head) if shift else head]
                pieces += [tile(base + t) for t in range(1, whole_tiles)]
                packed = None
                for k in range(fold):
                    value = tail[k * part : (k + 1) * part]
                    turn = (k * rest - shift) % LANES
                    if turn:
                        value = pltpu.roll(value, turn, 1)
                    packed = value if k == 0 else jnp.where(lane[:part] < k * rest, packed, value)
                pieces.append(packed)
                value = jnp.concatenate(pieces)
                relative = (QUAD * group + q) ^ chip
                outer, a, b = relative >> 2, (relative >> order[0]) & 1, (relative >> order[1]) & 1
                send, keep = outs[2 * index], outs[2 * index + 1]

                @pl.when(a == 1)
                def _():
                    send[b, outer, half] = value.astype(send.dtype)

                @pl.when(a == 0)
                def _():
                    keep[b, outer, half] = value

    for half in range(halves):
        for group in range(own.shape[2] // span):
            for load in loads[half, group]:
                load.wait()
            if groups <= 2:
                step(half, group, accs.at[group % 2])
            else:
                lax.fori_loop(0, groups, lambda g, c: step(half, g, accs.at[0]), None)


def project(spot, arrived, own, other, count_x, cuts, stages):
    block = own.shape[2] // count_x
    rows, depth = sum(t.shape[0] for t in arrived), own.shape[1]
    groups = count_x // QUAD
    if groups > 2 and own.shape[0] > 1:
        two = [project(spot, arrived, own[h : h + 1], other[h : h + 1], count_x, cuts, stages) for h in range(2)]
        return [jnp.concatenate(pair, axis=2) for pair in zip(*two)]
    shapes = []
    for first, last, _ in cuts:
        lines = count_x * (last - first) * block // LANES
        for kind in (wire_type(0, stages), jnp.float32):
            shapes.append(jax.ShapeDtypeStruct((2, groups, own.shape[0], lines, LANES), kind))
    inside = pl.BlockSpec(memory_space=pltpu.VMEM)
    scratch = jax.ShapeDtypeStruct((2, rows, QUAD * block), jnp.float32)
    held = sum(t.size * t.dtype.itemsize for t in [*arrived, *arrived, own, other, scratch, *shapes])
    return pl.pallas_call(
        functools.partial(project_kernel, block, cuts, len(arrived)),
        out_shape=shapes,
        in_specs=[pl.BlockSpec(memory_space=pltpu.SMEM)] + [inside] * len(arrived) + [pl.BlockSpec(memory_space=pltpu.HBM)] * 2,
        out_specs=[inside] * len(shapes),
        scratch_shapes=[
            pltpu.VMEM((rows, 2 * depth), arrived[0].dtype),
            pltpu.VMEM(own.shape, own.dtype),
            pltpu.VMEM(own.shape, own.dtype),
            pltpu.VMEM(scratch.shape, scratch.dtype),
            pltpu.SemaphoreType.DMA((2, own.shape[0], 2)),
        ],
        compiler_params=pltpu.CompilerParams(vmem_limit_bytes=max(held + 4 * 1024 * 1024, 44 * 1024 * 1024)),
        cost_estimate=pl.CostEstimate(
            flops=4 * rows * depth * own.shape[2], bytes_accessed=2 * own.size, transcendentals=0
        ),
    )(spot, *arrived, own, other)


def down_kernel(block, count, order, place_ref, keep_in, recv_in, own, other, send, keep, hidden):
    chip, core = place_ref[0], place_ref[1]
    whole_tiles, rest = block // LANES, block % LANES
    fold = LANES // rest

    @pl.when(pl.program_id(0) == 0)
    def _():
        gate = keep_in[0] + recv_in[0].astype(jnp.float32)
        upper = keep_in[1] + recv_in[1].astype(jnp.float32)
        value = gate / (1.0 + jnp.exp(-gate)) * upper
        tiles = jnp.concatenate(
            [value[piece * count : (piece + 1) * count] for piece in range(whole_tiles)], axis=1
        )
        shift = (chip & (QUAD - 1)) * rest
        turned = pltpu.roll(tiles, lax.rem(whole_tiles * LANES - shift, whole_tiles * LANES), 1)
        high = turned.astype(jnp.bfloat16)
        hidden[:count, : whole_tiles * LANES] = high
        hidden[count:, : whole_tiles * LANES] = (turned - high.astype(jnp.float32)).astype(jnp.bfloat16)
        packed = value[whole_tiles * count :]
        part = count // fold
        for k in range(fold):
            turned = pltpu.roll(packed, (LANES - k * rest) % LANES, 1) if k else packed
            turned = turned[:, :rest]
            high = turned.astype(jnp.bfloat16)
            hidden[k * part : (k + 1) * part, whole_tiles * LANES :] = high
            hidden[count + k * part : count + (k + 1) * part, whole_tiles * LANES :] = (
                turned - high.astype(jnp.float32)
            ).astype(jnp.bfloat16)

    low, high = hidden[:, : block // 2], hidden[:, block // 2 :]
    product = jnp.dot(
        jnp.where(core == 0, low, high), own[...], preferred_element_type=jnp.float32
    ) + jnp.dot(jnp.where(core == 0, high, low), other[...], preferred_element_type=jnp.float32)
    product = product[:count] + product[count:]
    chips = 4 * send.shape[1]
    each = count // chips
    for owner in range(chips):
        place(owner ^ lax.rem(chip, chips), order, send, keep, product[owner * each : (owner + 1) * each])


def down_project(spot, keep, recv, own, other, count, order, count_x, stages, span=(0, 1), wide=4096):
    block, features = 2 * own.shape[0], own.shape[1]
    part, parts = span
    features = features // parts
    wide = min(wide, features)
    groups = count_x // 2 // QUAD
    each = count // (count_x // 2)
    whole = pl.BlockSpec(keep.shape, lambda c, s: (0, 0, 0))
    out = pl.BlockSpec((2, groups, each, wide), lambda c, s: (0, 0, 0, c))
    weights = pl.BlockSpec((block // 2, wide), lambda c, s: (0, part * (features // wide) + c))
    return pl.pallas_call(
        functools.partial(down_kernel, block, count, order),
        out_shape=[
            jax.ShapeDtypeStruct((2, groups, each, features), kind)
            for kind in (wire_type(0, stages), jnp.float32)
        ],
        grid_spec=pltpu.PrefetchScalarGridSpec(
            num_scalar_prefetch=1,
            grid=(features // wide,),
            in_specs=[
                whole,
                whole,
                weights,
                weights,
            ],
            out_specs=[out, out],
            scratch_shapes=[pltpu.VMEM((2 * count, block), jnp.bfloat16)],
        ),
        compiler_params=pltpu.CompilerParams(
            vmem_limit_bytes=4 * block * wide + 20 * count * wide + 4 * 1024 * 1024
        ),
        cost_estimate=pl.CostEstimate(
            flops=2 * count * block * features, bytes_accessed=2 * block * features, transcendentals=0
        ),
    )(spot, keep, recv, own, other)


def swap(value, bit):
    count = lax.axis_size("gx")
    return lax.ppermute(value, "gx", [(i, i ^ (1 << bit)) for i in range(count)])


def swap_cores(value):
    return lax.ppermute(value, "gy", [(0, 1), (1, 0)])


def after(value, done):
    return value if done is None else lax.optimization_barrier((value, done))[0]


def halving(send, keep, order, count, stages, done):
    recv = swap(after(send, done), order[0])
    done = yield send
    for stage in range(1, count):
        acc = keep + after(recv, done).astype(jnp.float32)
        kind = wire_type(stage, stages)
        if stage == 1:
            send, keep, bit = acc[1].astype(kind), acc[0], order[1]
        else:
            half = acc.shape[0] // 2
            send, keep, bit = acc[half:].astype(kind), acc[:half], 1 + half.bit_length()
        recv = swap(send, bit)
        done = yield send
    return keep[0], after(recv, done)[0]


def move(value, pairs):
    return lax.ppermute(value, ("gx", "gy"), [(2 * a + b, 2 * c + d) for (a, b), (c, d) in pairs])


def chunk_steps(spot, flags, parts, downs, count, orders, count_x, stages):
    first_core, owner = flags
    done = yield
    keep, recv = yield from halving(parts[0], parts[1], orders[0], stages, stages, done)
    send, keep = down_project(spot, keep, recv, *downs, count, orders[1], count_x, stages)
    keep, recv = yield from halving(send, keep, orders[1], stages - 1, stages, None)
    acc = keep + recv.astype(jnp.float32)
    low, high = jnp.split(acc, 2, axis=1)
    mine, send = jnp.where(first_core, low, high), jnp.where(first_core, high, low)
    got = swap_cores(send)
    done = yield send
    got = after(got, done)
    send = jnp.where(owner, got, mine).astype(wire_type(stages - 1, stages))
    recv = swap(send, stages - 1)
    done = yield send
    result = (jnp.where(owner, mine, got) + after(recv, done).astype(jnp.float32)).astype(jnp.bfloat16)
    return result.reshape(2, result.shape[0] // 2, -1)


def local(tokens, gate_up, down_weight):
    count_x = lax.axis_size("gx")
    stages = count_x.bit_length() - 1
    chip, core = lax.axis_index("gx"), lax.axis_index("gy")
    spot = jnp.stack([chip, core]).astype(jnp.int32)
    each = tokens.shape[1]
    depth = gate_up.shape[1]

    half = count_x // 2
    other = swap_cores(gate_up)
    flags = core == 0, core == chip // half
    tokens, spot, *flags = lax.optimization_barrier((tokens, spot, *flags))
    dealt = deal(spot, tokens.reshape(2 * each, -1), half)
    arrived = [
        move(message, [((i, j), (j * half + (i + turn) % half, i // half)) for i in range(count_x) for j in range(2)])
        for turn, message in enumerate(dealt)
    ]
    down_other = swap_cores(after(down_weight, arrived))
    if 2 * each % 16:
        twice = jnp.stack(arrived[::-1] * 2)
        arrived = lax.dynamic_slice_in_dim(twice, half - 1 - lax.rem(chip, half), half)
        arrived = [arrived.reshape(half * 2 * each, -1)]

    if stages == 3 and each == 24:
        step, orders, turns = 8, ORDERS, TURNS
    else:
        step, orders = each, [((0, 1), (0, 1))]
        turns = [0] * (2 * stages + 2)
    cuts = tuple((i * step, (i + 1) * step, order[0]) for i, order in enumerate(orders))
    parts = project(spot, arrived, gate_up, other, count_x, cuts, stages)
    chunks = [
        chunk_steps(
            spot, flags, parts[2 * i : 2 * i + 2], (down_weight, down_other), count_x * step, order, count_x, stages
        )
        for i, order in enumerate(orders)
    ]
    for chunk in chunks:
        next(chunk)
    done, results = None, {}
    for i in turns:
        try:
            done = chunks[i].send(done)
        except StopIteration as end:
            results[i] = end.value
    return jnp.concatenate([results[i] for i in range(len(cuts))], axis=1)


def solution(mesh):
    return jax.shard_map(
        local,
        mesh=mesh,
        in_specs=(
            P(None, ("groups", "gx"), "gy"),
            P(None, ("gx", "gy"), None),
            P(("gx", "gy"), None),
        ),
        out_specs=P(None, ("groups", "gx"), "gy"),
        check_vma=False,
    )
```

```python
import functools

import jax
import jax.numpy as jnp
from jax import lax
from jax.experimental import pallas as pl
from jax.experimental.pallas import tpu as pltpu
from jax.sharding import PartitionSpec as P

LANES = 128
QUAD = 4


ORDERS = [(((0, 1),), ((0, 1), (1, 0))), (((1, 0),), ((0, 1), (1, 0))), (((0, 1), (1, 0)), ((0, 1), (1, 0)))]
TURNS = [0, 1, 0, 1, 2, 0, 1, 2, 0, 2, 1, 0, 2, 1, 0, 1, 0, 2, 1, 0, 2, 1, 2, 2]


def wire_type(stage, stages):
    return jnp.bfloat16 if stages - stage <= 3 else jnp.float32


def place(relative, order, send, keep, value):
    first = (relative >> order[0]) & 1
    second = (relative >> order[1]) & 1
    group = 0 if send.shape[1] == 1 else relative >> 2

    @pl.when(first == 1)
    def _():
        send[second, group] = value.astype(send.dtype)

    @pl.when(first == 0)
    def _():
        keep[second, group] = value


def deal_kernel(place_ref, tokens, *messages):
    count, wide = len(messages), messages[0].shape[1]
    for turn, message in enumerate(messages):
        target = lax.rem(place_ref[0] + turn, count)
        message[...] = tokens[:, pl.ds(pl.multiple_of(target * wide, LANES), wide)]


def deal(spot, tokens, count):
    rows, features = tokens.shape
    inside = pl.BlockSpec(memory_space=pltpu.VMEM)
    return pl.pallas_call(
        deal_kernel,
        out_shape=[jax.ShapeDtypeStruct((rows, features // count), tokens.dtype)] * count,
        in_specs=[pl.BlockSpec(memory_space=pltpu.SMEM), inside],
        out_specs=[inside] * count,
        compiler_params=pltpu.CompilerParams(vmem_limit_bytes=8 * 1024 * 1024),
    )(spot, tokens)


def project_kernel(block, cuts, messages, place_ref, *refs):
    arrived, own_in, other_in = refs[:messages], refs[messages], refs[messages + 1]
    outs, (tokens, own, other, accs, sems) = refs[messages + 2 : -5], refs[-5:]
    chip, core = place_ref[0], place_ref[1]
    chips, each = tokens.shape[0] // cuts[-1][1], cuts[-1][1]
    halves, depth, wide = own.shape[0], own.shape[1], QUAD * block
    groups = own.shape[2] // wide
    span = wide if groups <= 2 else own.shape[2]
    loads = {}
    for half in range(halves):
        for group in range(own.shape[2] // span):
            lanes = slice(group * span, (group + 1) * span)
            loads[half, group] = [
                pltpu.make_async_copy(source.at[half, :, lanes], target.at[half, :, lanes], sems.at[i, half, group])
                for i, (source, target) in enumerate(((own_in, own), (other_in, other)))
            ]
            for load in loads[half, group]:
                load.start()
    size = arrived[0].shape[0]
    for turn, message in enumerate(arrived):
        source = lax.rem(chip + messages - turn, messages) if messages > 1 else 0
        tokens[pl.ds(pl.multiple_of(source * size, size), size), :] = message[...]
    low, high = tokens[:, :depth], tokens[:, depth:]
    first_rows = jnp.where(core == 0, low, high)
    second_rows = jnp.where(core == 0, high, low)
    whole_tiles, rest = block // LANES, block % LANES
    fold = LANES // rest

    def step(half, group, acc):
        at = group * wide
        span = pl.ds(at if isinstance(at, int) else pl.multiple_of(at, LANES), wide)
        acc[...] = jnp.dot(first_rows, own[half, :, span], preferred_element_type=jnp.float32) + jnp.dot(
            second_rows, other[half, :, span], preferred_element_type=jnp.float32
        )
        slot = 0
        for first, last, orders in cuts:
            split = len(orders) > 1
            order = orders[half] if split else orders[0]
            pair = outs[slot + 2 * half * split :][:2]
            slot += 2 * len(orders)
            count = chips * (last - first)
            part = count // fold
            lane = lax.broadcasted_iota(jnp.int32, (count, LANES), 1)

            def tile(at):
                lanes = pl.ds(pl.multiple_of(at * LANES, LANES), LANES)
                if count == tokens.shape[0]:
                    return acc[:, lanes]
                return jnp.concatenate([acc[c * each + first : c * each + last, lanes] for c in range(chips)])

            for near in range(QUAD):
                q = near ^ (chip & (QUAD - 1))
                base, shift = q * whole_tiles, q * rest
                tail = tile(base + whole_tiles)
                pieces = [jnp.where(lane < shift, tail, tile(base))]
                pieces += [tile(base + t) for t in range(1, whole_tiles)]
                packed = None
                for k in range(fold):
                    turn = lax.rem(k * rest - shift + LANES, LANES)
                    value = pltpu.roll(tail[k * part : (k + 1) * part], turn, 1)
                    packed = value if k == 0 else jnp.where(lane[:part] < k * rest, packed, value)
                pieces.append(packed)
                value = jnp.concatenate(pieces)
                outer = group ^ (chip >> 2)
                target = pair[1 - ((near >> order[0]) & 1)]
                target[(near >> order[1]) & 1, outer, 0 if split else half] = value.astype(target.dtype)

    for half in range(halves):
        for group in range(own.shape[2] // span):
            for load in loads[half, group]:
                load.wait()
            if groups <= 2:
                step(half, group, accs.at[group % 2])
            else:
                lax.fori_loop(0, groups, lambda g, c: step(half, g, accs.at[0]), None)


def project(spot, arrived, own, other, count_x, cuts, stages):
    block = own.shape[2] // count_x
    rows, depth = sum(t.shape[0] for t in arrived), own.shape[1]
    groups = count_x // QUAD
    if groups > 2 and own.shape[0] > 1:
        two = [project(spot, arrived, own[h : h + 1], other[h : h + 1], count_x, cuts, stages) for h in range(2)]
        return [jnp.concatenate(pair, axis=2) for pair in zip(*two)]
    shapes = []
    for first, last, orders in cuts:
        lines = count_x * (last - first) * block // LANES
        halves = 1 if len(orders) > 1 else own.shape[0]
        for kind in (wire_type(0, stages), jnp.float32) * len(orders):
            shapes.append(jax.ShapeDtypeStruct((2, groups, halves, lines, LANES), kind))
    inside = pl.BlockSpec(memory_space=pltpu.VMEM)
    scratch = jax.ShapeDtypeStruct((2, rows, QUAD * block), jnp.float32)
    held = sum(t.size * t.dtype.itemsize for t in [*arrived, *arrived, own, other, scratch, *shapes])
    return pl.pallas_call(
        functools.partial(project_kernel, block, cuts, len(arrived)),
        out_shape=shapes,
        in_specs=[pl.BlockSpec(memory_space=pltpu.SMEM)] + [inside] * len(arrived) + [pl.BlockSpec(memory_space=pltpu.HBM)] * 2,
        out_specs=[inside] * len(shapes),
        scratch_shapes=[
            pltpu.VMEM((rows, 2 * depth), arrived[0].dtype),
            pltpu.VMEM(own.shape, own.dtype),
            pltpu.VMEM(own.shape, own.dtype),
            pltpu.VMEM(scratch.shape, scratch.dtype),
            pltpu.SemaphoreType.DMA((2, own.shape[0], 2)),
        ],
        compiler_params=pltpu.CompilerParams(vmem_limit_bytes=max(held + 4 * 1024 * 1024, 44 * 1024 * 1024)),
        cost_estimate=pl.CostEstimate(
            flops=4 * rows * depth * own.shape[2], bytes_accessed=2 * own.size, transcendentals=0
        ),
    )(spot, *arrived, own, other)


def down_kernel(block, count, order, place_ref, *refs):
    terms, (own, other, send, keep, hidden) = refs[:-5], refs[-5:]
    chip, core = place_ref[0], place_ref[1]
    whole_tiles, rest = block // LANES, block % LANES
    fold = LANES // rest

    chips = 4 * send.shape[1]
    each = count // chips

    def by_owner(value):
        if chips > 4:
            return value
        blocks = [value[i * each : (i + 1) * each] for i in range(4)]
        for bit in (1, 2):
            flip = (chip & bit) != 0
            blocks = [jnp.where(flip, blocks[i ^ bit], blocks[i]) for i in range(4)]
        return jnp.concatenate(blocks)

    @pl.when(pl.program_id(0) == 0)
    def _():
        gate = terms[0][0] + terms[1][0].astype(jnp.float32)
        last = terms[-1].shape[0] - 1
        upper = terms[-2][last] + terms[-1][last].astype(jnp.float32)
        value = gate / (1.0 + jnp.exp(-gate)) * upper
        tiles = jnp.concatenate(
            [value[piece * count : (piece + 1) * count] for piece in range(whole_tiles)], axis=1
        )
        shift = (chip & (QUAD - 1)) * rest
        turned = pltpu.roll(tiles, lax.rem(whole_tiles * LANES - shift, whole_tiles * LANES), 1)
        turned = by_owner(turned)
        high = turned.astype(jnp.bfloat16)
        hidden[:count, : whole_tiles * LANES] = high
        hidden[count:, : whole_tiles * LANES] = (turned - high.astype(jnp.float32)).astype(jnp.bfloat16)
        packed = value[whole_tiles * count :]
        part = count // fold
        turned = [pltpu.roll(packed, (LANES - k * rest) % LANES, 1) if k else packed for k in range(fold)]
        turned = by_owner(jnp.concatenate(turned))[:, :rest]
        high = turned.astype(jnp.bfloat16)
        hidden[:count, whole_tiles * LANES :] = high
        hidden[count:, whole_tiles * LANES :] = (turned - high.astype(jnp.float32)).astype(jnp.bfloat16)

    low, high = hidden[:, : block // 2], hidden[:, block // 2 :]
    product = jnp.dot(
        jnp.where(core == 0, low, high), own[...], preferred_element_type=jnp.float32
    ) + jnp.dot(jnp.where(core == 0, high, low), other[...], preferred_element_type=jnp.float32)
    product = product[:count] + product[count:]
    for owner in range(chips):
        value = product[owner * each : (owner + 1) * each]
        if chips > 4:
            place(owner ^ lax.rem(chip, chips), order, send, keep, value)
        else:
            target = send if (owner >> order[0]) & 1 else keep
            target[(owner >> order[1]) & 1, 0] = value.astype(target.dtype)


def down_project(spot, terms, own, other, count, order, count_x, stages, span=(0, 1), wide=4096):
    block, features = 2 * own.shape[0], own.shape[1]
    part, parts = span
    features = features // parts
    wide = min(wide, features)
    groups = count_x // 2 // QUAD
    each = count // (count_x // 2)
    out = pl.BlockSpec((2, groups, each, wide), lambda c, s: (0, 0, 0, c))
    weights = pl.BlockSpec((block // 2, wide), lambda c, s: (0, part * (features // wide) + c))
    return pl.pallas_call(
        functools.partial(down_kernel, block, count, order),
        out_shape=[
            jax.ShapeDtypeStruct((2, groups, each, features), kind)
            for kind in (wire_type(0, stages), jnp.float32)
        ],
        grid_spec=pltpu.PrefetchScalarGridSpec(
            num_scalar_prefetch=1,
            grid=(features // wide,),
            in_specs=[
                *[pl.BlockSpec(term.shape, lambda c, s: (0, 0, 0)) for term in terms],
                weights,
                weights,
            ],
            out_specs=[out, out],
            scratch_shapes=[pltpu.VMEM((2 * count, block), jnp.bfloat16)],
        ),
        compiler_params=pltpu.CompilerParams(
            vmem_limit_bytes=4 * block * wide + 20 * count * wide + 4 * 1024 * 1024
        ),
        cost_estimate=pl.CostEstimate(
            flops=2 * count * block * features, bytes_accessed=2 * block * features, transcendentals=0
        ),
    )(spot, *terms, own, other)


def swap(value, bit):
    count = lax.axis_size("gx")
    return lax.ppermute(value, "gx", [(i, i ^ (1 << bit)) for i in range(count)])


def swap_cores(value):
    return lax.ppermute(value, "gy", [(0, 1), (1, 0)])


def after(value, done):
    return value if done is None else lax.optimization_barrier((value, done))[0]


def halving(send, keep, order, count, stages, done):
    recv = swap(send if done is None else after(send, done), order[0])
    done = yield send
    for stage in range(1, count):
        acc = keep + after(recv, done).astype(jnp.float32)
        kind = wire_type(stage, stages)
        if stage == 1:
            send, keep, bit = acc[1].astype(kind), acc[0], order[1]
        else:
            half = acc.shape[0] // 2
            send, keep, bit = acc[half:].astype(kind), acc[:half], 1 + half.bit_length()
        recv = swap(send, bit)
        done = yield send
    return keep[0], after(recv, done)[0]


def move(value, pairs):
    return lax.ppermute(value, ("gx", "gy"), [(2 * a + b, 2 * c + d) for (a, b), (c, d) in pairs])


def together(ways):
    done, ends = None, []
    while len(ends) < len(ways):
        sent = []
        for way in ways:
            try:
                sent.append(way.send(done))
            except StopIteration as end:
                ends.append(end.value)
        if sent:
            done = yield sent
    return ends


def chunk_steps(spot, flags, parts, downs, count, orders, count_x, stages):
    first_core, owner = flags
    done = yield
    ways = [
        halving(parts[2 * i], parts[2 * i + 1], order, stages, stages, done) for i, order in enumerate(orders[0])
    ]
    terms = yield from together(ways)
    terms = [term for pair in terms for term in pair]
    ways = []
    for part, order in enumerate(orders[1]):
        span = (part, len(orders[1]))
        sent, kept = down_project(spot, terms, *downs, count, order, count_x, stages, span)
        ways.append(halving(sent, kept, order, stages - 1, stages, None))
    terms = yield from together(ways)
    sums = [keep + recv.astype(jnp.float32) for keep, recv in terms]
    low, high = jnp.split(sums[0], 2, axis=1) if len(sums) == 1 else sums
    mine, send = jnp.where(first_core, low, high), jnp.where(first_core, high, low)
    got = swap_cores(send)
    done = yield send
    got = after(got, done)
    send = jnp.where(owner, got, mine).astype(wire_type(stages - 1, stages))
    recv = swap(send, stages - 1)
    done = yield send
    result = (jnp.where(owner, mine, got) + after(recv, done).astype(jnp.float32)).astype(jnp.bfloat16)
    return result.reshape(2, result.shape[0] // 2, -1)


def local(tokens, gate_up, down_weight):
    count_x = lax.axis_size("gx")
    stages = count_x.bit_length() - 1
    chip, core = lax.axis_index("gx"), lax.axis_index("gy")
    spot = jnp.stack([chip, core]).astype(jnp.int32)
    each = tokens.shape[1]
    depth = gate_up.shape[1]

    half = count_x // 2
    other = swap_cores(gate_up)
    flags = core == 0, core == chip // half
    tokens, spot, *flags = lax.optimization_barrier((tokens, spot, *flags))
    dealt = deal(spot, tokens.reshape(2 * each, -1), half)
    arrived = [
        move(message, [((i, j), (j * half + (i + turn) % half, i // half)) for i in range(count_x) for j in range(2)])
        for turn, message in enumerate(dealt)
    ]
    down_other = swap_cores(after(down_weight, arrived))
    if 2 * each % 16:
        twice = jnp.stack(arrived[::-1] * 2)
        arrived = lax.dynamic_slice_in_dim(twice, half - 1 - lax.rem(chip, half), half)
        arrived = [arrived.reshape(half * 2 * each, -1)]

    if stages == 3 and each == 24:
        step, orders, turns = 8, ORDERS, TURNS
    else:
        step, orders = each, [(((0, 1),), ((0, 1),))]
        turns = [0] * (2 * stages + 2)
    cuts = tuple((i * step, (i + 1) * step, order[0]) for i, order in enumerate(orders))
    starts = [2 * sum(len(order[0]) for order in orders[:i]) for i in range(len(orders) + 1)]
    parts = project(spot, arrived, gate_up, other, count_x, cuts, stages)
    chunks = [
        chunk_steps(
            spot, flags, parts[starts[i] : starts[i + 1]], (down_weight, down_other), count_x * step, order, count_x, stages
        )
        for i, order in enumerate(orders)
    ]
    for chunk in chunks:
        next(chunk)
    done, results = None, {}
    for i in turns:
        try:
            done = chunks[i].send(done)
        except StopIteration as end:
            results[i] = end.value
    return jnp.concatenate([results[i] for i in range(len(cuts))], axis=1)


def solution(mesh):
    return jax.shard_map(
        local,
        mesh=mesh,
        in_specs=(
            P(None, ("groups", "gx"), "gy"),
            P(None, ("gx", "gy"), None),
            P(("gx", "gy"), None),
        ),
        out_specs=P(None, ("groups", "gx"), "gy"),
        check_vma=False,
    )
```

```python
import functools

import jax
import jax.numpy as jnp
from jax import lax
from jax.experimental import pallas as pl
from jax.experimental.pallas import tpu as pltpu
from jax.sharding import PartitionSpec as P

LANES = 128
QUAD = 4


ORDERS = [(((0, 1), (1, 0)), ((0, 1), (1, 0))), (((0, 1), (1, 0)), ((0, 1), (1, 0))), (((0, 1), (1, 0)), ((0, 1), (1, 0)))]
TURNS = [0, 1, 0, 1, 2, 0, 1, 2, 0, 1, 2, 0, 1, 2, 0, 1, 0, 2, 1, 0, 2, 1, 2, 2]


def wire_type(stage, stages):
    return jnp.bfloat16 if stages - stage <= 3 else jnp.float32


def place(relative, order, send, keep, value):
    first = (relative >> order[0]) & 1
    second = (relative >> order[1]) & 1
    group = 0 if send.shape[1] == 1 else relative >> 2

    @pl.when(first == 1)
    def _():
        send[second, group] = value.astype(send.dtype)

    @pl.when(first == 0)
    def _():
        keep[second, group] = value


def deal_kernel(place_ref, tokens, *messages):
    count, wide = len(messages), messages[0].shape[1]
    for turn, message in enumerate(messages):
        target = lax.rem(place_ref[0] + turn, count)
        message[...] = tokens[:, pl.ds(pl.multiple_of(target * wide, LANES), wide)]


def deal(spot, tokens, count):
    rows, features = tokens.shape
    inside = pl.BlockSpec(memory_space=pltpu.VMEM)
    return pl.pallas_call(
        deal_kernel,
        out_shape=[jax.ShapeDtypeStruct((rows, features // count), tokens.dtype)] * count,
        in_specs=[pl.BlockSpec(memory_space=pltpu.SMEM), inside],
        out_specs=[inside] * count,
        compiler_params=pltpu.CompilerParams(vmem_limit_bytes=8 * 1024 * 1024),
    )(spot, tokens)


def project_kernel(block, cuts, messages, place_ref, *refs):
    arrived, own_in, other_in = refs[:messages], refs[messages], refs[messages + 1]
    outs, (tokens, own, other, accs, sems) = refs[messages + 2 : -5], refs[-5:]
    chip, core = place_ref[0], place_ref[1]
    chips, each = tokens.shape[0] // cuts[-1][1], cuts[-1][1]
    halves, depth, wide = own.shape[0], own.shape[1], QUAD * block
    groups = own.shape[2] // wide
    span = wide if groups <= 2 else own.shape[2]
    loads = {}
    for half in range(halves):
        for group in range(own.shape[2] // span):
            lanes = slice(group * span, (group + 1) * span)
            loads[half, group] = [
                pltpu.make_async_copy(source.at[half, :, lanes], target.at[half, :, lanes], sems.at[i, half, group])
                for i, (source, target) in enumerate(((own_in, own), (other_in, other)))
            ]
            for load in loads[half, group]:
                load.start()
    size = arrived[0].shape[0]
    for turn, message in enumerate(arrived):
        source = lax.rem(chip + messages - turn, messages) if messages > 1 else 0
        tokens[pl.ds(pl.multiple_of(source * size, size), size), :] = message[...]
    low, high = tokens[:, :depth], tokens[:, depth:]
    first_rows = jnp.where(core == 0, low, high)
    second_rows = jnp.where(core == 0, high, low)
    whole_tiles, rest = block // LANES, block % LANES
    fold = LANES // rest

    def step(half, group, acc):
        at = group * wide
        span = pl.ds(at if isinstance(at, int) else pl.multiple_of(at, LANES), wide)
        acc[...] = jnp.dot(first_rows, own[half, :, span], preferred_element_type=jnp.float32) + jnp.dot(
            second_rows, other[half, :, span], preferred_element_type=jnp.float32
        )
        slot = 0
        for first, last, orders in cuts:
            split = len(orders) > 1
            order = orders[half] if split else orders[0]
            pair = outs[slot + 2 * half * split :][:2]
            slot += 2 * len(orders)
            count = chips * (last - first)
            part = count // fold
            lane = lax.broadcasted_iota(jnp.int32, (count, LANES), 1)

            def tile(at):
                lanes = pl.ds(pl.multiple_of(at * LANES, LANES), LANES)
                if count == tokens.shape[0]:
                    return acc[:, lanes]
                return jnp.concatenate([acc[c * each + first : c * each + last, lanes] for c in range(chips)])

            for near in range(QUAD):
                q = near ^ (chip & (QUAD - 1))
                base, shift = q * whole_tiles, q * rest
                tail = tile(base + whole_tiles)
                pieces = [jnp.where(lane < shift, tail, tile(base))]
                pieces += [tile(base + t) for t in range(1, whole_tiles)]
                packed = None
                for k in range(fold):
                    turn = lax.rem(k * rest - shift + LANES, LANES)
                    value = pltpu.roll(tail[k * part : (k + 1) * part], turn, 1)
                    packed = value if k == 0 else jnp.where(lane[:part] < k * rest, packed, value)
                pieces.append(packed)
                value = jnp.concatenate(pieces)
                outer = group ^ (chip >> 2)
                target = pair[1 - ((near >> order[0]) & 1)]
                target[(near >> order[1]) & 1, outer, 0 if split else half] = value.astype(target.dtype)

    for half in range(halves):
        for group in range(own.shape[2] // span):
            for load in loads[half, group]:
                load.wait()
            if groups <= 2:
                step(half, group, accs.at[group % 2])
            else:
                lax.fori_loop(0, groups, lambda g, c: step(half, g, accs.at[0]), None)


def project(spot, arrived, own, other, count_x, cuts, stages):
    block = own.shape[2] // count_x
    rows, depth = sum(t.shape[0] for t in arrived), own.shape[1]
    groups = count_x // QUAD
    if groups > 2 and own.shape[0] > 1:
        two = [project(spot, arrived, own[h : h + 1], other[h : h + 1], count_x, cuts, stages) for h in range(2)]
        return [jnp.concatenate(pair, axis=2) for pair in zip(*two)]
    shapes = []
    for first, last, orders in cuts:
        lines = count_x * (last - first) * block // LANES
        halves = 1 if len(orders) > 1 else own.shape[0]
        for kind in (wire_type(0, stages), jnp.float32) * len(orders):
            shapes.append(jax.ShapeDtypeStruct((2, groups, halves, lines, LANES), kind))
    inside = pl.BlockSpec(memory_space=pltpu.VMEM)
    scratch = jax.ShapeDtypeStruct((2, rows, QUAD * block), jnp.float32)
    held = sum(t.size * t.dtype.itemsize for t in [*arrived, *arrived, own, other, scratch, *shapes])
    return pl.pallas_call(
        functools.partial(project_kernel, block, cuts, len(arrived)),
        out_shape=shapes,
        in_specs=[pl.BlockSpec(memory_space=pltpu.SMEM)] + [inside] * len(arrived) + [pl.BlockSpec(memory_space=pltpu.HBM)] * 2,
        out_specs=[inside] * len(shapes),
        scratch_shapes=[
            pltpu.VMEM((rows, 2 * depth), arrived[0].dtype),
            pltpu.VMEM(own.shape, own.dtype),
            pltpu.VMEM(own.shape, own.dtype),
            pltpu.VMEM(scratch.shape, scratch.dtype),
            pltpu.SemaphoreType.DMA((2, own.shape[0], 2)),
        ],
        compiler_params=pltpu.CompilerParams(vmem_limit_bytes=max(held + 4 * 1024 * 1024, 44 * 1024 * 1024)),
        cost_estimate=pl.CostEstimate(
            flops=4 * rows * depth * own.shape[2], bytes_accessed=2 * own.size, transcendentals=0
        ),
    )(spot, *arrived, own, other)


def down_kernel(block, count, order, place_ref, *refs):
    terms, (own, other, send, keep, hidden) = refs[:-5], refs[-5:]
    chip, core = place_ref[0], place_ref[1]
    whole_tiles, rest = block // LANES, block % LANES
    fold = LANES // rest

    chips = 4 * send.shape[1]
    each = count // chips

    def by_owner(value):
        if chips > 4:
            return value
        blocks = [value[i * each : (i + 1) * each] for i in range(4)]
        for bit in (1, 2):
            flip = (chip & bit) != 0
            blocks = [jnp.where(flip, blocks[i ^ bit], blocks[i]) for i in range(4)]
        return jnp.concatenate(blocks)

    @pl.when(pl.program_id(0) == 0)
    def _():
        gate = terms[0][0] + terms[1][0].astype(jnp.float32)
        last = terms[-1].shape[0] - 1
        upper = terms[-2][last] + terms[-1][last].astype(jnp.float32)
        value = gate / (1.0 + jnp.exp(-gate)) * upper
        tiles = jnp.concatenate(
            [value[piece * count : (piece + 1) * count] for piece in range(whole_tiles)], axis=1
        )
        shift = (chip & (QUAD - 1)) * rest
        turned = pltpu.roll(tiles, lax.rem(whole_tiles * LANES - shift, whole_tiles * LANES), 1)
        turned = by_owner(turned)
        high = turned.astype(jnp.bfloat16)
        hidden[:count, : whole_tiles * LANES] = high
        hidden[count:, : whole_tiles * LANES] = (turned - high.astype(jnp.float32)).astype(jnp.bfloat16)
        packed = value[whole_tiles * count :]
        part = count // fold
        turned = [pltpu.roll(packed, (LANES - k * rest) % LANES, 1) if k else packed for k in range(fold)]
        turned = by_owner(jnp.concatenate(turned))[:, :rest]
        high = turned.astype(jnp.bfloat16)
        hidden[:count, whole_tiles * LANES :] = high
        hidden[count:, whole_tiles * LANES :] = (turned - high.astype(jnp.float32)).astype(jnp.bfloat16)

    low, high = hidden[:, : block // 2], hidden[:, block // 2 :]
    product = jnp.dot(
        jnp.where(core == 0, low, high), own[...], preferred_element_type=jnp.float32
    ) + jnp.dot(jnp.where(core == 0, high, low), other[...], preferred_element_type=jnp.float32)
    product = product[:count] + product[count:]
    for owner in range(chips):
        value = product[owner * each : (owner + 1) * each]
        if chips > 4:
            place(owner ^ lax.rem(chip, chips), order, send, keep, value)
        else:
            target = send if (owner >> order[0]) & 1 else keep
            target[(owner >> order[1]) & 1, 0] = value.astype(target.dtype)


def down_project(spot, terms, own, other, count, order, count_x, stages, span=(0, 1), wide=4096):
    block, features = 2 * own.shape[0], own.shape[1]
    part, parts = span
    features = features // parts
    wide = min(wide, features)
    groups = count_x // 2 // QUAD
    each = count // (count_x // 2)
    out = pl.BlockSpec((2, groups, each, wide), lambda c, s: (0, 0, 0, c))
    weights = pl.BlockSpec((block // 2, wide), lambda c, s: (0, part * (features // wide) + c))
    return pl.pallas_call(
        functools.partial(down_kernel, block, count, order),
        out_shape=[
            jax.ShapeDtypeStruct((2, groups, each, features), kind)
            for kind in (wire_type(0, stages), jnp.float32)
        ],
        grid_spec=pltpu.PrefetchScalarGridSpec(
            num_scalar_prefetch=1,
            grid=(features // wide,),
            in_specs=[
                *[pl.BlockSpec(term.shape, lambda c, s: (0, 0, 0)) for term in terms],
                weights,
                weights,
            ],
            out_specs=[out, out],
            scratch_shapes=[pltpu.VMEM((2 * count, block), jnp.bfloat16)],
        ),
        compiler_params=pltpu.CompilerParams(
            vmem_limit_bytes=4 * block * wide + 20 * count * wide + 4 * 1024 * 1024
        ),
        cost_estimate=pl.CostEstimate(
            flops=2 * count * block * features, bytes_accessed=2 * block * features, transcendentals=0
        ),
    )(spot, *terms, own, other)


def swap(value, bit):
    count = lax.axis_size("gx")
    return lax.ppermute(value, "gx", [(i, i ^ (1 << bit)) for i in range(count)])


def swap_cores(value):
    return lax.ppermute(value, "gy", [(0, 1), (1, 0)])


def after(value, done):
    return value if done is None else lax.optimization_barrier((value, done))[0]


def halving(send, keep, order, count, stages, done):
    recv = swap(send if done is None else after(send, done), order[0])
    done = yield send
    for stage in range(1, count):
        acc = keep + after(recv, done).astype(jnp.float32)
        kind = wire_type(stage, stages)
        if stage == 1:
            send, keep, bit = acc[1].astype(kind), acc[0], order[1]
        else:
            half = acc.shape[0] // 2
            send, keep, bit = acc[half:].astype(kind), acc[:half], 1 + half.bit_length()
        recv = swap(send, bit)
        done = yield send
    return keep[0], after(recv, done)[0]


def move(value, pairs):
    return lax.ppermute(value, ("gx", "gy"), [(2 * a + b, 2 * c + d) for (a, b), (c, d) in pairs])


def together(ways):
    done, ends = None, []
    while len(ends) < len(ways):
        sent = []
        for way in ways:
            try:
                sent.append(way.send(done))
            except StopIteration as end:
                ends.append(end.value)
        if sent:
            done = yield sent
    return ends


def chunk_steps(spot, flags, parts, downs, count, orders, count_x, stages):
    first_core, owner = flags
    done = yield
    ways = [
        halving(parts[2 * i], parts[2 * i + 1], order, stages, stages, done) for i, order in enumerate(orders[0])
    ]
    terms = yield from together(ways)
    terms = [term for pair in terms for term in pair]
    ways = []
    for part, order in enumerate(orders[1]):
        span = (part, len(orders[1]))
        sent, kept = down_project(spot, terms, *downs, count, order, count_x, stages, span)
        ways.append(halving(sent, kept, order, stages - 1, stages, None))
    terms = yield from together(ways)
    sums = [keep + recv.astype(jnp.float32) for keep, recv in terms]
    low, high = jnp.split(sums[0], 2, axis=1) if len(sums) == 1 else sums
    mine, send = jnp.where(first_core, low, high), jnp.where(first_core, high, low)
    got = swap_cores(send)
    done = yield send
    got = after(got, done)
    send = jnp.where(owner, got, mine).astype(wire_type(stages - 1, stages))
    recv = swap(send, stages - 1)
    done = yield send
    result = (jnp.where(owner, mine, got) + after(recv, done).astype(jnp.float32)).astype(jnp.bfloat16)
    return result.reshape(2, result.shape[0] // 2, -1)


def local(tokens, gate_up, down_weight):
    count_x = lax.axis_size("gx")
    stages = count_x.bit_length() - 1
    chip, core = lax.axis_index("gx"), lax.axis_index("gy")
    spot = jnp.stack([chip, core]).astype(jnp.int32)
    each = tokens.shape[1]
    depth = gate_up.shape[1]

    half = count_x // 2
    other = swap_cores(gate_up)
    flags = core == 0, core == chip // half
    tokens, spot, *flags = lax.optimization_barrier((tokens, spot, *flags))
    dealt = deal(spot, tokens.reshape(2 * each, -1), half)
    arrived = [
        move(message, [((i, j), (j * half + (i + turn) % half, i // half)) for i in range(count_x) for j in range(2)])
        for turn, message in enumerate(dealt)
    ]
    down_other = swap_cores(after(down_weight, arrived))
    if 2 * each % 16:
        twice = jnp.stack(arrived[::-1] * 2)
        arrived = lax.dynamic_slice_in_dim(twice, half - 1 - lax.rem(chip, half), half)
        arrived = [arrived.reshape(half * 2 * each, -1)]

    if stages == 3 and each == 24:
        step, orders, turns = 8, ORDERS, TURNS
    else:
        step, orders = each, [(((0, 1),), ((0, 1),))]
        turns = [0] * (2 * stages + 2)
    cuts = tuple((i * step, (i + 1) * step, order[0]) for i, order in enumerate(orders))
    starts = [2 * sum(len(order[0]) for order in orders[:i]) for i in range(len(orders) + 1)]
    parts = project(spot, arrived, gate_up, other, count_x, cuts, stages)
    chunks = [
        chunk_steps(
            spot, flags, parts[starts[i] : starts[i + 1]], (down_weight, down_other), count_x * step, order, count_x, stages
        )
        for i, order in enumerate(orders)
    ]
    for chunk in chunks:
        next(chunk)
    done, results = None, {}
    for i in turns:
        try:
            done = chunks[i].send(done)
        except StopIteration as end:
            results[i] = end.value
    return jnp.concatenate([results[i] for i in range(len(cuts))], axis=1)


def solution(mesh):
    return jax.shard_map(
        local,
        mesh=mesh,
        in_specs=(
            P(None, ("groups", "gx"), "gy"),
            P(None, ("gx", "gy"), None),
            P(("gx", "gy"), None),
        ),
        out_specs=P(None, ("groups", "gx"), "gy"),
        check_vma=False,
    )
```

```python
import functools

import jax
import jax.numpy as jnp
from jax import lax
from jax.experimental import pallas as pl
from jax.experimental.pallas import tpu as pltpu
from jax.sharding import PartitionSpec as P

LANES = 128
QUAD = 4


ORDERS = [(((0, 1), (1, 0)), ((0, 1), (1, 0))), (((0, 1), (1, 0)), ((0, 1), (1, 0))), (((0, 1), (1, 0)), ((0, 1), (1, 0)))]
TURNS = [0, 1, 0, 1, 2, 0, 1, 2, 0, 1, 2, 0, 1, 2, 0, 0, 1, 2, 0, 1, 2, 1, 2, 2]


def wire_type(stage, stages):
    return jnp.bfloat16 if stages - stage <= 3 else jnp.float32


def place(relative, order, send, keep, value):
    first = (relative >> order[0]) & 1
    second = (relative >> order[1]) & 1
    group = 0 if send.shape[1] == 1 else relative >> 2

    @pl.when(first == 1)
    def _():
        send[second, group] = value.astype(send.dtype)

    @pl.when(first == 0)
    def _():
        keep[second, group] = value


def deal_kernel(place_ref, tokens, *messages):
    count, wide = len(messages), messages[0].shape[1]
    for turn, message in enumerate(messages):
        target = lax.rem(place_ref[0] + turn, count)
        message[...] = tokens[:, pl.ds(pl.multiple_of(target * wide, LANES), wide)]


def deal(spot, tokens, count):
    rows, features = tokens.shape
    inside = pl.BlockSpec(memory_space=pltpu.VMEM)
    return pl.pallas_call(
        deal_kernel,
        out_shape=[jax.ShapeDtypeStruct((rows, features // count), tokens.dtype)] * count,
        in_specs=[pl.BlockSpec(memory_space=pltpu.SMEM), inside],
        out_specs=[inside] * count,
        compiler_params=pltpu.CompilerParams(vmem_limit_bytes=8 * 1024 * 1024),
    )(spot, tokens)


def project_kernel(block, cuts, messages, place_ref, *refs):
    arrived, own_in, other_in = refs[:messages], refs[messages], refs[messages + 1]
    outs, (tokens, own, other, accs, sems) = refs[messages + 2 : -5], refs[-5:]
    chip, core = place_ref[0], place_ref[1]
    chips, each = tokens.shape[0] // cuts[-1][1], cuts[-1][1]
    halves, depth, wide = own.shape[0], own.shape[1], QUAD * block
    groups = own.shape[2] // wide
    span = wide if groups <= 2 else own.shape[2]
    loads = {}
    for half in range(halves):
        for group in range(own.shape[2] // span):
            lanes = slice(group * span, (group + 1) * span)
            loads[half, group] = [
                pltpu.make_async_copy(source.at[half, :, lanes], target.at[half, :, lanes], sems.at[i, half, group])
                for i, (source, target) in enumerate(((own_in, own), (other_in, other)))
            ]
            for load in loads[half, group]:
                load.start()
    size = arrived[0].shape[0]
    for turn, message in enumerate(arrived):
        source = lax.rem(chip + messages - turn, messages) if messages > 1 else 0
        tokens[pl.ds(pl.multiple_of(source * size, size), size), :] = message[...]
    low, high = tokens[:, :depth], tokens[:, depth:]
    first_rows = jnp.where(core == 0, low, high)
    second_rows = jnp.where(core == 0, high, low)
    whole_tiles, rest = block // LANES, block % LANES
    fold = LANES // rest

    def step(half, group, acc):
        at = group * wide
        span = pl.ds(at if isinstance(at, int) else pl.multiple_of(at, LANES), wide)
        acc[...] = jnp.dot(first_rows, own[half, :, span], preferred_element_type=jnp.float32) + jnp.dot(
            second_rows, other[half, :, span], preferred_element_type=jnp.float32
        )
        slot = 0
        for first, last, orders in cuts:
            split = len(orders) > 1
            order = orders[half] if split else orders[0]
            pair = outs[slot + 2 * half * split :][:2]
            slot += 2 * len(orders)
            count = chips * (last - first)
            part = count // fold
            lane = lax.broadcasted_iota(jnp.int32, (count, LANES), 1)

            def tile(at):
                lanes = pl.ds(pl.multiple_of(at * LANES, LANES), LANES)
                if count == tokens.shape[0]:
                    return acc[:, lanes]
                return jnp.concatenate([acc[c * each + first : c * each + last, lanes] for c in range(chips)])

            for near in range(QUAD):
                q = near ^ (chip & (QUAD - 1))
                base, shift = q * whole_tiles, q * rest
                tail = tile(base + whole_tiles)
                pieces = [jnp.where(lane < shift, tail, tile(base))]
                pieces += [tile(base + t) for t in range(1, whole_tiles)]
                packed = None
                for k in range(fold):
                    turn = lax.rem(k * rest - shift + LANES, LANES)
                    value = pltpu.roll(tail[k * part : (k + 1) * part], turn, 1)
                    packed = value if k == 0 else jnp.where(lane[:part] < k * rest, packed, value)
                pieces.append(packed)
                value = jnp.concatenate(pieces)
                outer = group ^ (chip >> 2)
                target = pair[1 - ((near >> order[0]) & 1)]
                target[(near >> order[1]) & 1, outer, 0 if split else half] = value.astype(target.dtype)

    for half in range(halves):
        for group in range(own.shape[2] // span):
            for load in loads[half, group]:
                load.wait()
            if groups <= 2:
                step(half, group, accs.at[group % 2])
            else:
                lax.fori_loop(0, groups, lambda g, c: step(half, g, accs.at[0]), None)


def project(spot, arrived, own, other, count_x, cuts, stages):
    block = own.shape[2] // count_x
    rows, depth = sum(t.shape[0] for t in arrived), own.shape[1]
    groups = count_x // QUAD
    if groups > 2 and own.shape[0] > 1:
        two = [project(spot, arrived, own[h : h + 1], other[h : h + 1], count_x, cuts, stages) for h in range(2)]
        return [jnp.concatenate(pair, axis=2) for pair in zip(*two)]
    shapes = []
    for first, last, orders in cuts:
        lines = count_x * (last - first) * block // LANES
        halves = 1 if len(orders) > 1 else own.shape[0]
        for kind in (wire_type(0, stages), jnp.float32) * len(orders):
            shapes.append(jax.ShapeDtypeStruct((2, groups, halves, lines, LANES), kind))
    inside = pl.BlockSpec(memory_space=pltpu.VMEM)
    scratch = jax.ShapeDtypeStruct((2, rows, QUAD * block), jnp.float32)
    held = sum(t.size * t.dtype.itemsize for t in [*arrived, *arrived, own, other, scratch, *shapes])
    return pl.pallas_call(
        functools.partial(project_kernel, block, cuts, len(arrived)),
        out_shape=shapes,
        in_specs=[pl.BlockSpec(memory_space=pltpu.SMEM)] + [inside] * len(arrived) + [pl.BlockSpec(memory_space=pltpu.HBM)] * 2,
        out_specs=[inside] * len(shapes),
        scratch_shapes=[
            pltpu.VMEM((rows, 2 * depth), arrived[0].dtype),
            pltpu.VMEM(own.shape, own.dtype),
            pltpu.VMEM(own.shape, own.dtype),
            pltpu.VMEM(scratch.shape, scratch.dtype),
            pltpu.SemaphoreType.DMA((2, own.shape[0], 2)),
        ],
        compiler_params=pltpu.CompilerParams(vmem_limit_bytes=max(held + 4 * 1024 * 1024, 44 * 1024 * 1024)),
        cost_estimate=pl.CostEstimate(
            flops=4 * rows * depth * own.shape[2], bytes_accessed=2 * own.size, transcendentals=0
        ),
    )(spot, *arrived, own, other)


def down_kernel(block, count, order, place_ref, *refs):
    terms, (own, other, send, keep, hidden) = refs[:-5], refs[-5:]
    chip, core = place_ref[0], place_ref[1]
    whole_tiles, rest = block // LANES, block % LANES
    fold = LANES // rest

    chips = 4 * send.shape[1]
    each = count // chips

    def by_owner(value):
        if chips > 4:
            return value
        blocks = [value[i * each : (i + 1) * each] for i in range(4)]
        for bit in (1, 2):
            flip = (chip & bit) != 0
            blocks = [jnp.where(flip, blocks[i ^ bit], blocks[i]) for i in range(4)]
        return jnp.concatenate(blocks)

    @pl.when(pl.program_id(0) == 0)
    def _():
        gate = terms[0][0] + terms[1][0].astype(jnp.float32)
        last = terms[-1].shape[0] - 1
        upper = terms[-2][last] + terms[-1][last].astype(jnp.float32)
        value = gate / (1.0 + jnp.exp(-gate)) * upper
        tiles = jnp.concatenate(
            [value[piece * count : (piece + 1) * count] for piece in range(whole_tiles)], axis=1
        )
        shift = (chip & (QUAD - 1)) * rest
        turned = pltpu.roll(tiles, lax.rem(whole_tiles * LANES - shift, whole_tiles * LANES), 1)
        turned = by_owner(turned)
        high = turned.astype(jnp.bfloat16)
        hidden[:count, : whole_tiles * LANES] = high
        hidden[count:, : whole_tiles * LANES] = (turned - high.astype(jnp.float32)).astype(jnp.bfloat16)
        packed = value[whole_tiles * count :]
        part = count // fold
        turned = [pltpu.roll(packed, (LANES - k * rest) % LANES, 1) if k else packed for k in range(fold)]
        turned = by_owner(jnp.concatenate(turned))[:, :rest]
        high = turned.astype(jnp.bfloat16)
        hidden[:count, whole_tiles * LANES :] = high
        hidden[count:, whole_tiles * LANES :] = (turned - high.astype(jnp.float32)).astype(jnp.bfloat16)

    low, high = hidden[:, : block // 2], hidden[:, block // 2 :]
    product = jnp.dot(
        jnp.where(core == 0, low, high), own[...], preferred_element_type=jnp.float32
    ) + jnp.dot(jnp.where(core == 0, high, low), other[...], preferred_element_type=jnp.float32)
    product = product[:count] + product[count:]
    for owner in range(chips):
        value = product[owner * each : (owner + 1) * each]
        if chips > 4:
            place(owner ^ lax.rem(chip, chips), order, send, keep, value)
        else:
            target = send if (owner >> order[0]) & 1 else keep
            target[(owner >> order[1]) & 1, 0] = value.astype(target.dtype)


def down_project(spot, terms, own, other, count, order, count_x, stages, span=(0, 1), wide=4096):
    block, features = 2 * own.shape[0], own.shape[1]
    part, parts = span
    features = features // parts
    wide = min(wide, features)
    groups = count_x // 2 // QUAD
    each = count // (count_x // 2)
    out = pl.BlockSpec((2, groups, each, wide), lambda c, s: (0, 0, 0, c))
    weights = pl.BlockSpec((block // 2, wide), lambda c, s: (0, part * (features // wide) + c))
    return pl.pallas_call(
        functools.partial(down_kernel, block, count, order),
        out_shape=[
            jax.ShapeDtypeStruct((2, groups, each, features), kind)
            for kind in (wire_type(0, stages), jnp.float32)
        ],
        grid_spec=pltpu.PrefetchScalarGridSpec(
            num_scalar_prefetch=1,
            grid=(features // wide,),
            in_specs=[
                *[pl.BlockSpec(term.shape, lambda c, s: (0, 0, 0)) for term in terms],
                weights,
                weights,
            ],
            out_specs=[out, out],
            scratch_shapes=[pltpu.VMEM((2 * count, block), jnp.bfloat16)],
        ),
        compiler_params=pltpu.CompilerParams(
            vmem_limit_bytes=4 * block * wide + 20 * count * wide + 4 * 1024 * 1024
        ),
        cost_estimate=pl.CostEstimate(
            flops=2 * count * block * features, bytes_accessed=2 * block * features, transcendentals=0
        ),
    )(spot, *terms, own, other)


def swap(value, bit):
    count = lax.axis_size("gx")
    return lax.ppermute(value, "gx", [(i, i ^ (1 << bit)) for i in range(count)])


def swap_cores(value):
    return lax.ppermute(value, "gy", [(0, 1), (1, 0)])


def after(value, done):
    return value if done is None else lax.optimization_barrier((value, done))[0]


def halving(send, keep, order, count, stages, done):
    recv = swap(send if done is None else after(send, done), order[0])
    done = yield send
    for stage in range(1, count):
        acc = keep + after(recv, done).astype(jnp.float32)
        kind = wire_type(stage, stages)
        if stage == 1:
            send, keep, bit = acc[1].astype(kind), acc[0], order[1]
        else:
            half = acc.shape[0] // 2
            send, keep, bit = acc[half:].astype(kind), acc[:half], 1 + half.bit_length()
        recv = swap(send, bit)
        done = yield send
    return keep[0], after(recv, done)[0]


def move(value, pairs):
    return lax.ppermute(value, ("gx", "gy"), [(2 * a + b, 2 * c + d) for (a, b), (c, d) in pairs])


def together(ways):
    done, ends = None, []
    while len(ends) < len(ways):
        sent = []
        for way in ways:
            try:
                sent.append(way.send(done))
            except StopIteration as end:
                ends.append(end.value)
        if sent:
            done = yield sent
    return ends


def chunk_steps(spot, flags, parts, downs, count, orders, count_x, stages):
    first_core, owner = flags
    done = yield
    ways = [
        halving(parts[2 * i], parts[2 * i + 1], order, stages, stages, done) for i, order in enumerate(orders[0])
    ]
    terms = yield from together(ways)
    terms = [term for pair in terms for term in pair]
    ways = []
    for part, order in enumerate(orders[1]):
        span = (part, len(orders[1]))
        sent, kept = down_project(spot, terms, *downs, count, order, count_x, stages, span)
        ways.append(halving(sent, kept, order, stages - 1, stages, None))
    terms = yield from together(ways)
    sums = [keep + recv.astype(jnp.float32) for keep, recv in terms]
    low, high = jnp.split(sums[0], 2, axis=1) if len(sums) == 1 else sums
    mine, send = jnp.where(first_core, low, high), jnp.where(first_core, high, low)
    got = swap_cores(send)
    done = yield send
    got = after(got, done)
    send = jnp.where(owner, got, mine).astype(wire_type(stages - 1, stages))
    recv = swap(send, stages - 1)
    done = yield send
    result = (jnp.where(owner, mine, got) + after(recv, done).astype(jnp.float32)).astype(jnp.bfloat16)
    return result.reshape(2, result.shape[0] // 2, -1)


def local(tokens, gate_up, down_weight):
    count_x = lax.axis_size("gx")
    stages = count_x.bit_length() - 1
    chip, core = lax.axis_index("gx"), lax.axis_index("gy")
    spot = jnp.stack([chip, core]).astype(jnp.int32)
    each = tokens.shape[1]
    depth = gate_up.shape[1]

    half = count_x // 2
    other = swap_cores(gate_up)
    flags = core == 0, core == chip // half
    tokens, spot, *flags = lax.optimization_barrier((tokens, spot, *flags))
    dealt = deal(spot, tokens.reshape(2 * each, -1), half)
    arrived = [
        move(message, [((i, j), (j * half + (i + turn) % half, i // half)) for i in range(count_x) for j in range(2)])
        for turn, message in enumerate(dealt)
    ]
    down_other = swap_cores(after(down_weight, arrived))
    if 2 * each % 16:
        twice = jnp.stack(arrived[::-1] * 2)
        arrived = lax.dynamic_slice_in_dim(twice, half - 1 - lax.rem(chip, half), half)
        arrived = [arrived.reshape(half * 2 * each, -1)]

    if stages == 3 and each == 24:
        step, orders, turns = 8, ORDERS, TURNS
    else:
        step, orders = each, [(((0, 1),), ((0, 1),))]
        turns = [0] * (2 * stages + 2)
    cuts = tuple((i * step, (i + 1) * step, order[0]) for i, order in enumerate(orders))
    starts = [2 * sum(len(order[0]) for order in orders[:i]) for i in range(len(orders) + 1)]
    parts = project(spot, arrived, gate_up, other, count_x, cuts, stages)
    chunks = [
        chunk_steps(
            spot, flags, parts[starts[i] : starts[i + 1]], (down_weight, down_other), count_x * step, order, count_x, stages
        )
        for i, order in enumerate(orders)
    ]
    for chunk in chunks:
        next(chunk)
    done, results = None, {}
    for i in turns:
        try:
            done = chunks[i].send(done)
        except StopIteration as end:
            results[i] = end.value
    return jnp.concatenate([results[i] for i in range(len(cuts))], axis=1)


def solution(mesh):
    return jax.shard_map(
        local,
        mesh=mesh,
        in_specs=(
            P(None, ("groups", "gx"), "gy"),
            P(None, ("gx", "gy"), None),
            P(("gx", "gy"), None),
        ),
        out_specs=P(None, ("groups", "gx"), "gy"),
        check_vma=False,
    )
```
